128 devices in a mesh: grp: 2 (over core), aux: 32 (over y, z_hi, x), tr: 2 (over z_lo).
Axes of the slice: x: 4, y: 4, z: 4 (z_hi: 2, z_lo: 2; z = z_hi * 2 + z_lo), core: 2. Of those that a mesh axis runs over, the one named last changes fastest.
Arguments:
- trial_vectors: float32 [64, 8, 512], P('aux', None, 'tr'), may hold values from -6 to 6
- energy_val: float32 [64], P('aux'), may hold values from -1 to -0.2
- energy_cond: float32 [512], P('tr'), may hold values from 0.2 to 2
- coef_occ: bfloat16 [2048, 64, 64], P('aux'), may hold values from -0.75 to 0.75
- coef_virt: bfloat16 [2048, 512, 512], P('aux', 'tr'), may hold values from -0.005859375 to 0.005859375
- pair_coef: bfloat16 [64, 512, 2048], P('aux', 'tr'), may hold values from -0.03125 to 0.03125
- live_aux: int32 [32], P('aux'), may hold values from 16 to 64, as said below
Outputs:
- applied: float32 [64, 8, 512], P('aux', None, 'tr')
- intersection: float32 [8, 8], replicated
The draws below stay inside these ranges and needn't reach their ends.
Inputs may be any that keep to these rules, and one draw needn't show every extreme that they name: `live_aux`: equals 64 on at least one shard.
All inputs are finite; a program needn't handle non-finite values.
Results may differ from the reference program's by a relative error of at most 0.0048.
Values may be sent and summed in bfloat16 or wider, within the bound.
No kernel may reach another device: no remote copies, remote signals or barrier semaphores. Data moves between devices by JAX's collectives and lax.ppermute only.
A program may use at most 64 MiB of HBM per device.

```python
import jax
import jax.numpy as jnp
from jax import lax

V = 64
C = 512
K = 8
PD = 64
NSHARD = 32
NAUX = 2048


def draw_live_aux(key, part):
    counts = jax.random.randint(jax.random.fold_in(key, 17), (NSHARD,), PD // 4, PD + 1)
    chosen = jax.random.randint(jax.random.fold_in(key, 29), (), 0, NSHARD)
    return counts.at[chosen].set(PD).astype(jnp.int32)


def block_scale(rng, dims, cuts, least, top_value):
    def one(dim, shards_of):
        draws = jax.random.uniform(jax.random.fold_in(jax.random.fold_in(rng, 6), dim), (shards_of,), jnp.float32, least / len(cuts), top_value / len(cuts))
        return jnp.repeat(jnp.exp(draws), dims[dim] // shards_of).reshape((-1,) + (1,) * (len(dims) - dim - 1))

    loudness = one(*cuts[0])
    for cut in cuts[1:]:
        loudness = loudness * one(*cut)
    return loudness


def bell_draw(key, shape, deviation, bound, cuts=(), held_as=jnp.bfloat16):
    loudness = block_scale(key, shape, cuts, -0.22, 0.18) if cuts else 1.0
    drawn = jax.random.normal(key, shape, jnp.float32) * deviation * loudness
    return jnp.minimum(jnp.maximum(drawn, -bound), bound).astype(held_as)


def setup_inputs(seed: int = 0) -> dict:
    streams_of = jax.random.split(jax.random.key(seed), 8)
    trial_vectors = bell_draw(streams_of[0], (V, K, C), 1.0, 6.0, ((0, 32), (2, 2)), jnp.float32)
    energy_val = jnp.clip(-1.0 + 0.8 * jax.random.uniform(streams_of[1], (V,), jnp.float32) ** block_scale(streams_of[1], (V,), ((0, 32),), -0.2, 0.2), -1.0, -0.2)
    energy_cond = jnp.clip(0.2 + 1.8 * jax.random.uniform(streams_of[2], (C,), jnp.float32) ** block_scale(streams_of[2], (C,), ((0, 2),), -0.2, 0.2), 0.2, 2.0)
    coef_occ = bell_draw(streams_of[3], (NAUX, V, V), V ** -0.5, 0.75, ((0, 32),))
    coef_virt = bell_draw(streams_of[4], (NAUX, C, C), (C * NAUX) ** -0.5, 0.005859375, ((0, 32), (1, 2)))
    pair_coef = bell_draw(streams_of[5], (V, C, NAUX), (V * C) ** -0.5, 0.03125, ((0, 32), (1, 2)))
    live_aux = draw_live_aux(jax.random.fold_in(streams_of[7], 71), 0)
    return dict(trial_vectors=trial_vectors, energy_val=energy_val, energy_cond=energy_cond, coef_occ=coef_occ, coef_virt=coef_virt, pair_coef=pair_coef, live_aux=live_aux)


def apply_hamiltonian(vectors, energy_gap, coef_occ, coef_virt, pair_coef, live_aux):
    rounded = vectors.astype(jnp.bfloat16)
    rounded_wide = rounded.astype(jnp.float32)

    def one_shard(running, shard_index):
        block_occ = lax.dynamic_slice_in_dim(coef_occ, shard_index * PD, PD, 0).astype(jnp.float32)
        block_virt = lax.dynamic_slice_in_dim(coef_virt, shard_index * PD, PD, 0).astype(jnp.float32)
        keep_mask = (jnp.arange(PD, dtype=jnp.int32) < live_aux[shard_index]).astype(jnp.float32)
        blended = jnp.einsum('puv,vkc->pukc', block_occ, rounded_wide)
        blended = (blended * keep_mask[:, None, None, None]).astype(jnp.bfloat16)
        running = running + jnp.einsum('pukc,pcd->ukd', blended.astype(jnp.float32), block_virt)
        return running, None

    zero_term = jnp.zeros((V, K, C), jnp.float32)
    direct_term, _ = lax.scan(one_shard, zero_term, jnp.arange(NSHARD, dtype=jnp.int32))
    pair_wide = pair_coef.astype(jnp.float32)
    projection = jnp.einsum('vcp,vkc->kp', pair_wide, rounded_wide)
    projection_b = projection.astype(jnp.bfloat16)
    exchange_term = jnp.einsum('vcp,kp->vkc', pair_wide, projection_b.astype(jnp.float32))
    return energy_gap[:, None, :] * vectors + direct_term + exchange_term


def reference(trial_vectors, energy_val, energy_cond, coef_occ, coef_virt, pair_coef, live_aux):
    energy_gap = energy_cond[None, :] - energy_val[:, None]
    applied_first = apply_hamiltonian(trial_vectors, energy_gap, coef_occ, coef_virt, pair_coef, live_aux)
    intersection = jnp.einsum('vkc,vjc->kj', trial_vectors, applied_first, precision=lax.Precision.HIGHEST) / (V * C)
    residual = applied_first - jnp.einsum('vkc,kj->vjc', trial_vectors, intersection, precision=lax.Precision.HIGHEST)
    correction = residual / energy_gap[:, None, :]
    applied = apply_hamiltonian(correction, energy_gap, coef_occ, coef_virt, pair_coef, live_aux)
    return applied, intersection
```

```python
import functools

import jax
import jax.numpy as jnp
from jax import lax
from jax.experimental import pallas as pl
from jax.experimental.pallas import tpu as pltpu
from jax.sharding import PartitionSpec as P

V = 64
C = 512
K = 8
HALF = 4
AUX = 32
TR = 2
CB = C // TR
PAIRS = AUX * TR
SLOTS = 64
NAUX = 2048
BLOCK = 8
TILES = NAUX // 128
F32 = jnp.float32
BF16 = jnp.bfloat16
VMEM = pl.BlockSpec(memory_space=pltpu.VMEM)
SMEM = pl.BlockSpec(memory_space=pltpu.SMEM)
NT = (((1,), (1,)), ((), ()))


def params(mib):
    return pltpu.CompilerParams(vmem_limit_bytes=mib * 2**20)


def dot(a, b):
    return jnp.dot(a, b, preferred_element_type=F32)


def lane_ids(shape):
    return lax.broadcasted_iota(jnp.int32, shape, len(shape) - 1)


def own_rows(core, rows):
    return jnp.where(core == 0, rows[:HALF], rows[HALF:])


def first_kernel(trial_ref, pair_ref, out_ref):
    rounded = [trial_ref[v].astype(BF16) for v in range(2)]
    wide = jnp.concatenate(rounded, axis=1)
    projection = dot(wide, pair_ref[...]).astype(BF16)
    for device in range(PAIRS):
        tile = device // 4
        out_ref[device, :, : 2 * CB] = wide
        out_ref[device, :, 2 * CB :] = projection[:, 128 * tile : 128 * tile + 128]


def direct_kernel(first, *refs):
    if first:
        (
            where_ref, live_ref, arrived_ref, occ_ref, virt_ref, trial_ref, gap_ref,
            out_ref, rows_ref, vectors_ref, blended_ref, total_ref,
        ) = refs
    else:
        (
            where_ref, live_ref, arrived_ref, occ_ref, virt_ref,
            out_ref, rows_ref, vectors_ref, blended_ref, total_ref,
        ) = refs
    step = pl.program_id(0)
    core, aux, tr = where_ref[0], where_ref[1], where_ref[2]

    @pl.when(step == 0)
    def _():
        total_ref[...] = jnp.zeros_like(total_ref)
        if first:
            for a in range(AUX):
                for t in range(TR):
                    slab = arrived_ref[2 * a + t].astype(F32)
                    for u in range(2):
                        for q in range(2):
                            at = CB * u + 128 * q
                            rows_ref[t, q, 16 * a + 8 * u : 16 * a + 8 * u + 8, :] = slab[:, at : at + 128]
            for k in range(HALF):
                for q in range(2):
                    part = rows_ref[tr, q, pl.ds(HALF * core + k, V, stride=K), :]
                    vectors_ref[k, :, 128 * q : 128 * q + 128] = part.astype(BF16)
        else:
            for a in range(AUX):
                for q in range(2):
                    part = arrived_ref[a, :, 128 * q : 128 * q + 128]
                    rows_ref[0, q, 8 * a : 8 * a + 8, :] = part.astype(F32)
            for k in range(HALF):
                for q in range(2):
                    part = rows_ref[0, q, pl.ds(k, V, stride=HALF), :]
                    vectors_ref[k, :, 128 * q : 128 * q + 128] = part.astype(BF16)

    occ = occ_ref[...].reshape(BLOCK * V, V)
    live = live_ref[0] - step * BLOCK
    slot = lax.broadcasted_iota(jnp.int32, (BLOCK * V, 1), 0) // V
    keep = (slot < live).astype(F32)
    for k in range(HALF):
        piece = (dot(occ, vectors_ref[k]) * keep).astype(BF16)
        for p in range(BLOCK):
            blended_ref[V * k : V * k + V, CB * p : CB * p + CB] = piece[V * p : V * p + V]
    product = dot(blended_ref[...], virt_ref[...])
    for q in range(C // 128):
        total_ref[q] += product[:, 128 * q : 128 * q + 128]

    @pl.when(step == SLOTS // BLOCK - 1)
    def _():
        if first:
            shares = jnp.zeros((K, HALF * V), F32)
            for t in range(TR):
                product = lax.dot_general(
                    jnp.concatenate([rows_ref[t, q] for q in range(2)], axis=1).astype(BF16),
                    jnp.concatenate([total_ref[2 * t + q] for q in range(2)], axis=1).astype(BF16),
                    NT,
                    preferred_element_type=F32,
                ).reshape(V, K, HALF * V)
                mine = lax.broadcasted_iota(jnp.int32, product.shape, 0)
                theirs = lane_ids(product.shape) % V
                shares += jnp.where(mine == theirs, product, 0.0).sum(axis=0)
            group = lane_ids(shares.shape) // V
            lanes = lane_ids((K, 128))
            kept = jnp.zeros((K, 128), F32)
            for j in range(HALF):
                column = jnp.where(group == j, shares, 0.0).sum(axis=1, keepdims=True)
                for v in range(2):
                    vectors = trial_ref[v]
                    other = own_rows(core, vectors)[j : j + 1] * gap_ref[v : v + 1]
                    column += (vectors * other).sum(axis=1, keepdims=True)
                high = column.astype(BF16).astype(F32)
                kept = jnp.where(lanes % 32 == j, high, kept)
                kept = jnp.where(lanes % 32 == HALF + j, column - high, kept)
            projection = jnp.zeros((K, 128), F32)
            for device in range(PAIRS):
                projection += arrived_ref[device, :, 2 * CB :].astype(F32)
            quarter = (TR * aux + tr) % 4
            extra = jnp.where(lanes // 32 == quarter, projection, kept)
        else:
            extra = jnp.zeros((K, 128), F32)
            for a in range(AUX):
                extra += arrived_ref[a, :, CB:].astype(F32)
        extra = extra.astype(BF16)
        for a in range(AUX):
            for t in range(TR):
                for q in range(2):
                    part = [
                        total_ref[2 * t + q, pl.ds(2 * a + u, HALF, stride=V), :]
                        for u in range(2)
                    ]
                    part = jnp.concatenate(part, axis=0).astype(BF16)
                    out_ref[2 * a + t, :, 128 * q : 128 * q + 128] = part
                out_ref[2 * a + t, :, CB:] = extra


def both_valence(rows):
    wide = (HALF, rows.shape[1])
    return jnp.concatenate(
        [jnp.broadcast_to(rows[v : v + 1], wide) for v in range(2)], axis=0
    )


def direct_sum(arrived_ref):
    total = jnp.zeros((2 * HALF, CB), F32)
    for device in range(PAIRS):
        total += arrived_ref[device, :, :CB].astype(F32)
    return total


def middle_kernel(
    where_ref, arrived_ref, pair_ref, trial_ref, gap_ref, out_ref, correction_ref, meet_ref
):
    core = where_ref[0]
    direct = direct_sum(arrived_ref)
    lanes = lane_ids((K, 128))
    tiles = []
    sums = [jnp.zeros((K, 128), F32) for _ in range(4)]
    for tile in range(TILES):
        whole = jnp.zeros((K, 128), F32)
        for quarter in range(4):
            extra = arrived_ref[4 * tile + quarter, :, CB:].astype(F32)
            whole = jnp.where(lanes // 32 == quarter, extra, whole)
            sums[quarter] += extra
        tiles.append(whole.astype(BF16))
    projection = jnp.concatenate(tiles, axis=1)
    exchange_full = lax.dot_general(projection, pair_ref[...], NT, preferred_element_type=F32)
    mine = own_rows(core, exchange_full)
    exchange = jnp.concatenate([mine[:, :CB], mine[:, CB:]], axis=0)
    shares = jnp.zeros((K, 128), F32)
    for quarter in range(4):
        shares += jnp.where(lanes // 32 == (quarter + 1) % 4, sums[quarter], 0.0)
    meet_exchange = lax.dot_general(projection, projection, NT, preferred_element_type=F32)
    meet = []
    for j in range(HALF):
        column = jnp.where(lanes % 32 % HALF == j, jnp.where(lanes % 32 < K, shares, 0.0), 0.0)
        column = column.sum(axis=1, keepdims=True)
        own = jnp.where(core == 0, meet_exchange[:, j : j + 1], meet_exchange[:, HALF + j : HALF + j + 1])
        meet.append((column + own) / (V * C))
    kept = jnp.zeros((K, 128), F32)
    for j in range(HALF):
        kept = jnp.where(lanes == j, meet[j], kept)
    meet_ref[...] = kept
    gap = both_valence(gap_ref[...])
    vectors = [trial_ref[v] for v in range(2)]
    trial = jnp.concatenate([own_rows(core, vectors[v]) for v in range(2)], axis=0)
    applied = gap * trial + direct + exchange
    overlap = jnp.concatenate(
        [(vectors[v] * meet[j]).sum(axis=0, keepdims=True) for v in range(2) for j in range(HALF)],
        axis=0,
    )
    correction = (applied - overlap) / gap
    correction_ref[...] = correction
    rounded = correction.astype(BF16)
    wide = jnp.concatenate([correction[:HALF], correction[HALF:]], axis=1)
    wide = jnp.concatenate([wide, jnp.zeros_like(wide)], axis=0).astype(BF16)
    projection = dot(wide, pair_ref[...]).astype(BF16)
    for a in range(AUX):
        tile = a // 2
        out_ref[a, :, :CB] = rounded
        out_ref[a, :, CB:] = projection[:, 128 * tile : 128 * tile + 128]


def last_kernel(arrived_ref, pair_ref, correction_ref, gap_ref, out_ref):
    direct = direct_sum(arrived_ref)
    tiles = []
    for tile in range(TILES):
        whole = arrived_ref[4 * tile, :, CB:].astype(F32) + arrived_ref[4 * tile + 1, :, CB:].astype(F32)
        tiles.append(whole.astype(BF16))
    projection = jnp.concatenate(tiles, axis=1)
    exchange = lax.dot_general(projection, pair_ref[...], NT, preferred_element_type=F32)
    exchange = jnp.concatenate([exchange[:HALF, :CB], exchange[:HALF, CB:]], axis=0)
    out_ref[...] = both_valence(gap_ref[...]) * correction_ref[...] + direct + exchange


def direct_call(first, where, live, arrived, occ, virt, *local):
    whole = [VMEM] * len(local)
    rows = (TR, 2, V * K, 128) if first else (1, 2, V * HALF, 128)
    return pl.pallas_call(
        functools.partial(direct_kernel, first),
        grid=(SLOTS // BLOCK,),
        in_specs=[
            SMEM,
            SMEM,
            VMEM,
            pl.BlockSpec((BLOCK, V, V), lambda i: (i, 0, 0)),
            pl.BlockSpec((BLOCK * CB, C), lambda i: (i, 0)),
            *whole,
        ],
        out_specs=VMEM,
        out_shape=jax.ShapeDtypeStruct((PAIRS, 2 * HALF, CB + 128), BF16),
        scratch_shapes=[
            pltpu.VMEM(rows, F32),
            pltpu.VMEM((HALF, V, CB), BF16),
            pltpu.VMEM((HALF * V, BLOCK * CB), BF16),
            pltpu.VMEM((C // 128, HALF * V, 128), F32),
        ],
        compiler_params=params(32),
    )(where, live, arrived, occ, virt, *local)


def body(trial_vectors, energy_val, energy_cond, coef_occ, coef_virt, pair_coef, live_aux):
    where = jnp.stack([lax.axis_index("grp"), lax.axis_index("aux"), lax.axis_index("tr")])
    where = where.astype(jnp.int32)
    gap = energy_cond[None, :] - energy_val[:, None]
    pair = pair_coef.reshape(2 * CB, NAUX)
    virt = coef_virt.reshape(SLOTS * CB, C)

    def exchange(x, axes):
        return lax.all_to_all(x, axes, split_axis=0, concat_axis=0, tiled=True)

    sent = pl.pallas_call(
        first_kernel,
        in_specs=[VMEM, VMEM],
        out_specs=VMEM,
        out_shape=jax.ShapeDtypeStruct((PAIRS, K, 2 * CB + 128), BF16),
        compiler_params=params(16),
    )(trial_vectors, pair)
    arrived = exchange(sent, ("aux", "tr"))
    sent = direct_call(True, where, live_aux, arrived, coef_occ, virt, trial_vectors, gap)
    arrived = exchange(sent, ("aux", "tr"))
    sent, correction, meet = pl.pallas_call(
        middle_kernel,
        in_specs=[SMEM] + [VMEM] * 4,
        out_specs=[VMEM] * 3,
        out_shape=[
            jax.ShapeDtypeStruct((AUX, 2 * HALF, CB + 128), BF16),
            jax.ShapeDtypeStruct((2 * HALF, CB), F32),
            jax.ShapeDtypeStruct((K, 128), F32),
        ],
        compiler_params=params(16),
    )(where, arrived, pair, trial_vectors, gap)
    arrived = exchange(sent, ("aux",))
    sent = direct_call(False, where, live_aux, arrived, coef_occ, virt)
    arrived = exchange(sent, ("aux", "tr"))
    applied = pl.pallas_call(
        last_kernel,
        in_specs=[VMEM] * 4,
        out_specs=VMEM,
        out_shape=jax.ShapeDtypeStruct((2 * HALF, CB), F32),
        compiler_params=params(16),
    )(arrived, pair, correction, gap)
    both = lax.all_gather(jnp.concatenate([applied, meet], axis=1), "grp")
    applied = both[:, :, :CB].reshape(2, 2, HALF, CB).transpose(1, 0, 2, 3).reshape(2, K, CB)
    intersection = jnp.concatenate([both[0, :, CB : CB + HALF], both[1, :, CB : CB + HALF]], axis=1)
    return (applied, intersection)


def solution(mesh):
    in_specs = (
        P("aux", None, "tr"),
        P("aux"),
        P("tr"),
        P("aux", None, None),
        P("aux", "tr", None),
        P("aux", "tr", None),
        P("aux"),
    )
    out_specs = (P("aux", None, "tr"), P())
    return jax.shard_map(body, mesh=mesh, in_specs=in_specs, out_specs=out_specs, check_vma=False)
```

```python
import functools

import jax
import jax.numpy as jnp
from jax import lax
from jax.experimental import pallas as pl
from jax.experimental.pallas import tpu as pltpu
from jax.sharding import PartitionSpec as P

V = 64
C = 512
K = 8
HALF = 4
AUX = 32
TR = 2
CB = C // TR
PAIRS = AUX * TR
SLOTS = 64
NAUX = 2048
BLOCK = 8
STEPS = SLOTS // BLOCK
AHEAD = 2
PARTS = 4
TILES = NAUX // 128
F32 = jnp.float32
BF16 = jnp.bfloat16
VMEM = pl.BlockSpec(memory_space=pltpu.VMEM)
SMEM = pl.BlockSpec(memory_space=pltpu.SMEM)
HBM = pl.BlockSpec(memory_space=pltpu.HBM)
NT = (((1,), (1,)), ((), ()))


def stays(x):
    return pltpu.with_memory_space_constraint(x, pltpu.HBM)


def params(mib):
    return pltpu.CompilerParams(vmem_limit_bytes=mib * 2**20)


def dot(a, b):
    return jnp.dot(a, b, preferred_element_type=F32)


def lane_ids(shape):
    return lax.broadcasted_iota(jnp.int32, shape, len(shape) - 1)


def own_rows(core, rows):
    return jnp.where(core == 0, rows[:HALF], rows[HALF:])


def both_halves(rows):
    return jnp.concatenate([rows[:, :CB], rows[:, CB:]], axis=0)


def first_kernel(
    trial_hbm, pair_hbm, cond_hbm, val_hbm, out_ref, trial_ref, gap_ref, pair_ref, cond_ref, val_ref, sems
):
    parts = [pl.ds(NAUX // PARTS * i, NAUX // PARTS) for i in range(PARTS)]
    copies = [
        pltpu.make_async_copy(trial_hbm, trial_ref, sems.at[0]),
        pltpu.make_async_copy(cond_hbm, cond_ref, sems.at[1]),
        pltpu.make_async_copy(val_hbm, val_ref, sems.at[2]),
    ]
    for i in range(PARTS):
        copies.append(pltpu.make_async_copy(pair_hbm.at[:, parts[i]], pair_ref.at[:, parts[i]], sems.at[3 + i]))
    for copy in copies:
        copy.start()
    copies[0].wait()
    wide = jnp.concatenate([trial_ref[v].astype(BF16) for v in range(2)], axis=1)
    for device in range(PAIRS):
        out_ref[device, :, : 2 * CB] = wide
    copies[1].wait()
    copies[2].wait()
    for v in range(2):
        gap_ref[HALF * v : HALF * v + HALF] = jnp.broadcast_to(cond_ref[...] - val_ref[v], (HALF, CB))
    for i in range(PARTS):
        copies[3 + i].wait()
        projection = dot(wide, pair_ref[:, parts[i]]).astype(BF16)
        for tile in range(TILES // PARTS):
            for device in range(4):
                at = 4 * (TILES // PARTS * i + tile) + device
                out_ref[at, :, 2 * CB :] = projection[:, 128 * tile : 128 * tile + 128]


def direct_kernel(first, *refs):
    if first:
        live_ref, arrived_ref, occ_hbm, virt_hbm, trial_ref, gap_ref = refs[:6]
        out_ref, occ_ref, virt_ref, rows_ref, vectors_ref, blended_ref, total_ref, sems = refs[6:]
    else:
        live_ref, arrived_ref, occ_ref, virt_ref = refs[:4]
        out_ref, vectors_ref, blended_ref, total_ref = refs[4:]
    core, aux, tr = lax.axis_index("grp"), lax.axis_index("aux"), lax.axis_index("tr")

    def fetch_occ(step):
        slots = pl.ds(step * BLOCK, BLOCK)
        return pltpu.make_async_copy(occ_hbm.at[slots], occ_ref.at[slots], sems.at[0, step])

    def fetch_virt(step):
        rows = pl.ds(step * BLOCK * CB, BLOCK * CB)
        return pltpu.make_async_copy(virt_hbm.at[rows], virt_ref.at[rows], sems.at[1, step])

    if first:
        for step in range(AHEAD):
            fetch_occ(step).start()
            fetch_virt(step).start()

    row = lax.broadcasted_iota(jnp.int32, (HALF * V, 1), 0)
    if first:
        for a in range(AUX):
            for t in range(TR):
                slab = arrived_ref[2 * a + t, :, : 2 * CB].astype(F32)
                rows_ref[t, 16 * a : 16 * a + 16] = both_halves(slab).astype(BF16)
        chosen = lax.broadcasted_iota(jnp.int32, (HALF * V, K * V), 1)
        wanted = K * (row % V) + HALF * core + row // V
        wide = rows_ref[tr]
    else:
        chosen = lax.broadcasted_iota(jnp.int32, (HALF * V, HALF * V), 1)
        wanted = HALF * (row % V) + row // V
        wide = arrived_ref[:, :, :CB].astype(F32).reshape(HALF * V, CB).astype(BF16)
    vectors_ref[...] = dot((chosen == wanted).astype(BF16), wide).astype(BF16)

    live = live_ref[0]
    slot = lax.broadcasted_iota(jnp.int32, (BLOCK * V, V), 0) // V

    def blend(step):
        occ = occ_ref[BLOCK * step : BLOCK * step + BLOCK].reshape(BLOCK * V, V)
        occ = jnp.where(slot < live - step * BLOCK, occ, jnp.zeros_like(occ))
        for k in range(HALF):
            piece = dot(occ, vectors_ref[V * k : V * k + V]).astype(BF16)
            for p in range(BLOCK):
                blended_ref[step % 2, V * k : V * k + V, CB * p : CB * p + CB] = piece[V * p : V * p + V]

    if first:
        fetch_occ(0).wait()
    blend(0)
    for step in range(STEPS):
        if first:
            fetch_virt(step).wait()
            if step + AHEAD < STEPS:
                fetch_occ(step + AHEAD).start()
                fetch_virt(step + AHEAD).start()
        rows = slice(step * BLOCK * CB, (step + 1) * BLOCK * CB)
        product = dot(blended_ref[step % 2], virt_ref[rows])
        if step + 1 < STEPS:
            if first:
                fetch_occ(step + 1).wait()
            blend(step + 1)
        if step == 0:
            total_ref[...] = product
        else:
            total_ref[...] += product

    lanes = lane_ids((K, 128))
    total = total_ref[...].astype(BF16)
    chosen = lax.broadcasted_iota(jnp.int32, (HALF * V, HALF * V), 1)
    owned = dot((chosen == V * (row % HALF) + row // HALF).astype(BF16), total).astype(BF16).astype(F32)
    if first:
        shares = jnp.zeros((K, HALF * V), F32)
        for t in range(TR):
            product = lax.dot_general(
                rows_ref[t], total[:, CB * t : CB * t + CB], NT, preferred_element_type=F32
            ).reshape(V, K, HALF * V)
            mine = lax.broadcasted_iota(jnp.int32, product.shape, 0)
            theirs = lane_ids(product.shape) % V
            shares += jnp.where(mine == theirs, product, 0.0).sum(axis=0)
        group = lane_ids(shares.shape) // V
        kept = jnp.zeros((K, 128), F32)
        for j in range(HALF):
            column = jnp.where(group == j, shares, 0.0).sum(axis=1, keepdims=True)
            for v in range(2):
                vectors = trial_ref[v]
                other = own_rows(core, vectors)[j : j + 1] * gap_ref[HALF * v : HALF * v + 1]
                column += (vectors * other).sum(axis=1, keepdims=True)
            high = column.astype(BF16).astype(F32)
            kept = jnp.where(lanes % 32 == j, high, kept)
            kept = jnp.where(lanes % 32 == HALF + j, column - high, kept)
        projection = jnp.zeros((K, 128), F32)
        for device in range(PAIRS):
            projection += arrived_ref[device, :, 2 * CB :].astype(F32)
        quarter = (TR * aux + tr) % 4
        extra = jnp.where(lanes // 32 == quarter, projection, kept)
    else:
        extra = jnp.zeros((K, 128), F32)
        for a in range(AUX):
            extra += arrived_ref[a, :, CB:].astype(F32)
    extra = extra.astype(BF16)
    for a in range(AUX):
        for t in range(TR):
            out_ref[2 * a + t, :, :CB] = owned[8 * a : 8 * a + 8, CB * t : CB * t + CB].astype(BF16)
            out_ref[2 * a + t, :, CB:] = extra


def direct_sum(arrived_ref):
    total = jnp.zeros((2 * HALF, CB), F32)
    for device in range(PAIRS):
        total += arrived_ref[device, :, :CB].astype(F32)
    return total


def middle_kernel(
    arrived_ref, pair_ref, trial_ref, gap_ref, out_ref, correction_ref, meet_ref
):
    core = lax.axis_index("grp")
    direct = direct_sum(arrived_ref)
    lanes = lane_ids((K, 128))
    tiles = []
    sums = [jnp.zeros((K, 128), F32) for _ in range(4)]
    for tile in range(TILES):
        whole = jnp.zeros((K, 128), F32)
        for quarter in range(4):
            extra = arrived_ref[4 * tile + quarter, :, CB:].astype(F32)
            whole = jnp.where(lanes // 32 == quarter, extra, whole)
            sums[quarter] += extra
        tiles.append(whole.astype(BF16))
    projection = jnp.concatenate(tiles, axis=1)
    exchange_full = lax.dot_general(projection, pair_ref[...], NT, preferred_element_type=F32)
    mine = own_rows(core, exchange_full)
    exchange = jnp.concatenate([mine[:, :CB], mine[:, CB:]], axis=0)
    shares = jnp.zeros((K, 128), F32)
    for quarter in range(4):
        shares += jnp.where(lanes // 32 == (quarter + 1) % 4, sums[quarter], 0.0)
    meet_exchange = lax.dot_general(projection, projection, NT, preferred_element_type=F32)
    meet = []
    for j in range(HALF):
        column = jnp.where(lanes % 32 % HALF == j, jnp.where(lanes % 32 < K, shares, 0.0), 0.0)
        column = column.sum(axis=1, keepdims=True)
        own = jnp.where(core == 0, meet_exchange[:, j : j + 1], meet_exchange[:, HALF + j : HALF + j + 1])
        meet.append((column + own) / (V * C))
    kept = jnp.zeros((K, 128), F32)
    for j in range(HALF):
        kept = jnp.where(lanes == j, meet[j], kept)
    meet_ref[...] = kept
    gap = gap_ref[...]
    vectors = [trial_ref[v] for v in range(2)]
    trial = jnp.concatenate([own_rows(core, vectors[v]) for v in range(2)], axis=0)
    applied = gap * trial + direct + exchange
    overlap = jnp.concatenate(
        [(vectors[v] * meet[j]).sum(axis=0, keepdims=True) for v in range(2) for j in range(HALF)],
        axis=0,
    )
    correction = (applied - overlap) / gap
    correction_ref[...] = correction
    rounded = correction.astype(BF16)
    wide = jnp.concatenate([correction[:HALF], correction[HALF:]], axis=1)
    wide = jnp.concatenate([wide, jnp.zeros_like(wide)], axis=0).astype(BF16)
    projection = dot(wide, pair_ref[...]).astype(BF16)
    for a in range(AUX):
        tile = a // 2
        out_ref[a, :, :CB] = rounded
        out_ref[a, :, CB:] = projection[:, 128 * tile : 128 * tile + 128]


def last_kernel(arrived_ref, pair_ref, correction_ref, gap_ref, out_ref):
    direct = direct_sum(arrived_ref)
    tiles = []
    for tile in range(TILES):
        whole = arrived_ref[4 * tile, :, CB:].astype(F32) + arrived_ref[4 * tile + 1, :, CB:].astype(F32)
        tiles.append(whole.astype(BF16))
    projection = jnp.concatenate(tiles, axis=1)
    exchange = lax.dot_general(projection, pair_ref[...], NT, preferred_element_type=F32)
    exchange = jnp.concatenate([exchange[:HALF, :CB], exchange[:HALF, CB:]], axis=0)
    out_ref[...] = gap_ref[...] * correction_ref[...] + direct + exchange


def direct_call(first, live, arrived, occ, virt, *local):
    out = jax.ShapeDtypeStruct((PAIRS, 2 * HALF, CB + 128), BF16)
    scratch = [
        pltpu.VMEM((HALF * V, CB), BF16),
        pltpu.VMEM((2, HALF * V, BLOCK * CB), BF16),
        pltpu.VMEM((HALF * V, C), F32),
    ]
    if first:
        scratch = [pltpu.VMEM((TR, K * V, CB), BF16), *scratch, pltpu.SemaphoreType.DMA((2, STEPS))]
    return pl.pallas_call(
        functools.partial(direct_kernel, first),
        in_specs=[SMEM, VMEM, HBM, HBM, VMEM, VMEM] if first else [SMEM, VMEM, VMEM, VMEM],
        out_specs=[VMEM] * 3 if first else VMEM,
        out_shape=[out, jax.typeof(occ), jax.typeof(virt)] if first else out,
        scratch_shapes=scratch,
        compiler_params=params(30 if first else 12),
    )(live, arrived, *((stays(occ), stays(virt)) if first else (occ, virt)), *local)


def body(trial_vectors, energy_val, energy_cond, coef_occ, coef_virt, pair_coef, live_aux):
    pair = pair_coef.reshape(2 * CB, NAUX)
    virt = coef_virt.reshape(SLOTS * CB, C)
    cond = energy_cond.reshape(1, CB)

    def exchange(x, axes):
        return lax.all_to_all(x, axes, split_axis=0, concat_axis=0, tiled=True)

    sent, trial, gap, pair = pl.pallas_call(
        first_kernel,
        in_specs=[HBM] * 4,
        out_specs=[VMEM] * 4,
        out_shape=[
            jax.ShapeDtypeStruct((PAIRS, K, 2 * CB + 128), BF16),
            jax.ShapeDtypeStruct((2, K, CB), F32),
            jax.ShapeDtypeStruct((2 * HALF, CB), F32),
            jax.typeof(pair),
        ],
        scratch_shapes=[
            pltpu.VMEM((1, CB), F32),
            pltpu.SMEM((2,), F32),
            pltpu.SemaphoreType.DMA((3 + PARTS,)),
        ],
        compiler_params=params(8),
    )(*(stays(x) for x in (trial_vectors, pair, cond, energy_val)))
    arrived = exchange(sent, ("aux", "tr"))
    sent, occ, virt = direct_call(True, live_aux, arrived, coef_occ, virt, trial, gap)
    arrived = exchange(sent, ("aux", "tr"))
    sent, correction, meet = pl.pallas_call(
        middle_kernel,
        in_specs=[VMEM] * 4,
        out_specs=[VMEM] * 3,
        out_shape=[
            jax.ShapeDtypeStruct((AUX, 2 * HALF, CB + 128), BF16),
            jax.ShapeDtypeStruct((2 * HALF, CB), F32),
            jax.ShapeDtypeStruct((K, 128), F32),
        ],
        compiler_params=params(8),
    )(arrived, pair, trial, gap)
    arrived = exchange(sent, ("aux",))
    sent = direct_call(False, live_aux, arrived, occ, virt)
    arrived = exchange(sent, ("aux", "tr"))
    applied = pl.pallas_call(
        last_kernel,
        in_specs=[VMEM] * 4,
        out_specs=VMEM,
        out_shape=jax.ShapeDtypeStruct((2 * HALF, CB), F32),
        compiler_params=params(8),
    )(arrived, pair, correction, gap)
    both = lax.all_gather(jnp.concatenate([applied, meet], axis=1), "grp")
    applied = both[:, :, :CB].reshape(2, 2, HALF, CB).transpose(1, 0, 2, 3).reshape(2, K, CB)
    intersection = jnp.concatenate([both[0, :, CB : CB + HALF], both[1, :, CB : CB + HALF]], axis=1)
    return (applied, intersection)


def solution(mesh):
    in_specs = (
        P("aux", None, "tr"),
        P("aux"),
        P("tr"),
        P("aux", None, None),
        P("aux", "tr", None),
        P("aux", "tr", None),
        P("aux"),
    )
    out_specs = (P("aux", None, "tr"), P())
    return jax.shard_map(body, mesh=mesh, in_specs=in_specs, out_specs=out_specs, check_vma=False)
```

```python
import functools

import jax
import jax.numpy as jnp
from jax import lax
from jax.experimental import pallas as pl
from jax.experimental.pallas import tpu as pltpu
from jax.sharding import PartitionSpec as P

V = 64
C = 512
K = 8
HALF = 4
AUX = 32
TR = 2
CB = C // TR
PAIRS = AUX * TR
SLOTS = 64
NAUX = 2048
BLOCK = 8
STEPS = SLOTS // BLOCK
PARTS = 4
UNTIL_DIRECT = 2 * 10**10
TILES = NAUX // 128
F32 = jnp.float32
BF16 = jnp.bfloat16
VMEM = pl.BlockSpec(memory_space=pltpu.VMEM)
SMEM = pl.BlockSpec(memory_space=pltpu.SMEM)
HBM = pl.BlockSpec(memory_space=pltpu.HBM)
NT = (((1,), (1,)), ((), ()))


def stays(x):
    return pltpu.with_memory_space_constraint(x, pltpu.HBM)


def params(mib):
    return pltpu.CompilerParams(vmem_limit_bytes=mib * 2**20)


def dot(a, b):
    return jnp.dot(a, b, preferred_element_type=F32)


def lane_ids(shape):
    return lax.broadcasted_iota(jnp.int32, shape, len(shape) - 1)


def own_rows(core, rows):
    return jnp.where(core == 0, rows[:HALF], rows[HALF:])


def both_halves(rows):
    return jnp.concatenate([rows[:, :CB], rows[:, CB:]], axis=0)


def first_kernel(
    live_ref, trial_hbm, pair_hbm, cond_hbm, val_hbm, out_ref, trial_ref, gap_ref, pair_ref, cond_ref, val_ref, sems
):
    parts = [pl.ds(NAUX // PARTS * i, NAUX // PARTS) for i in range(PARTS)]
    copies = [
        pltpu.make_async_copy(trial_hbm, trial_ref, sems.at[0]),
        pltpu.make_async_copy(cond_hbm, cond_ref, sems.at[1]),
        pltpu.make_async_copy(val_hbm, val_ref, sems.at[2]),
    ]
    for i in range(PARTS):
        copies.append(pltpu.make_async_copy(pair_hbm.at[:, parts[i]], pair_ref.at[:, parts[i]], sems.at[3 + i]))
    for copy in copies:
        copy.start()
    copies[0].wait()
    wide = jnp.concatenate([trial_ref[v].astype(BF16) for v in range(2)], axis=1)
    for device in range(PAIRS):
        out_ref[device, :, : 2 * CB] = wide
    copies[1].wait()
    copies[2].wait()
    for v in range(2):
        gap_ref[HALF * v : HALF * v + HALF] = jnp.broadcast_to(cond_ref[...] - val_ref[v], (HALF, CB))
    for i in range(PARTS):
        copies[3 + i].wait()
        projection = dot(wide, pair_ref[:, parts[i]]).astype(BF16)
        for tile in range(TILES // PARTS):
            for device in range(4):
                at = 4 * (TILES // PARTS * i + tile) + device
                out_ref[at, :, 2 * CB :] = projection[:, 128 * tile : 128 * tile + 128]


def direct_kernel(first, *refs):
    if first:
        live_ref, arrived_ref, occ_ref, virt_ref, trial_ref, gap_ref = refs[:6]
        out_ref, rows_ref, vectors_ref, blended_ref, total_ref = refs[6:]
    else:
        live_ref, arrived_ref, occ_ref, virt_ref = refs[:4]
        out_ref, vectors_ref, blended_ref, total_ref = refs[4:]
    core, aux, tr = lax.axis_index("grp"), lax.axis_index("aux"), lax.axis_index("tr")

    row = lax.broadcasted_iota(jnp.int32, (HALF * V, 1), 0)
    if first:
        for a in range(AUX):
            for t in range(TR):
                slab = arrived_ref[2 * a + t, :, : 2 * CB].astype(F32)
                rows_ref[t, 16 * a : 16 * a + 16] = both_halves(slab).astype(BF16)
        chosen = lax.broadcasted_iota(jnp.int32, (HALF * V, K * V), 1)
        wanted = K * (row % V) + HALF * core + row // V
        wide = rows_ref[tr]
    else:
        chosen = lax.broadcasted_iota(jnp.int32, (HALF * V, HALF * V), 1)
        wanted = HALF * (row % V) + row // V
        wide = arrived_ref[:, :, :CB].astype(F32).reshape(HALF * V, CB).astype(BF16)
    vectors_ref[...] = dot((chosen == wanted).astype(BF16), wide).astype(BF16)

    live = live_ref[0]
    slot = lax.broadcasted_iota(jnp.int32, (BLOCK * V, V), 0) // V

    def blend(step):
        occ = occ_ref[BLOCK * step : BLOCK * step + BLOCK].reshape(BLOCK * V, V)
        occ = jnp.where(slot < live - step * BLOCK, occ, jnp.zeros_like(occ))
        for k in range(HALF):
            piece = dot(occ, vectors_ref[V * k : V * k + V]).astype(BF16)
            for p in range(BLOCK):
                blended_ref[step % 2, V * k : V * k + V, CB * p : CB * p + CB] = piece[V * p : V * p + V]

    blend(0)
    for step in range(STEPS):
        rows = slice(step * BLOCK * CB, (step + 1) * BLOCK * CB)
        product = dot(blended_ref[step % 2], virt_ref[rows])
        if step + 1 < STEPS:
            blend(step + 1)
        if step == 0:
            total_ref[...] = product
        else:
            total_ref[...] += product

    lanes = lane_ids((K, 128))
    total = total_ref[...].astype(BF16)
    chosen = lax.broadcasted_iota(jnp.int32, (HALF * V, HALF * V), 1)
    owned = dot((chosen == V * (row % HALF) + row // HALF).astype(BF16), total).astype(BF16).astype(F32)
    if first:
        shares = jnp.zeros((K, HALF * V), F32)
        for t in range(TR):
            product = lax.dot_general(
                rows_ref[t], total[:, CB * t : CB * t + CB], NT, preferred_element_type=F32
            ).reshape(V, K, HALF * V)
            mine = lax.broadcasted_iota(jnp.int32, product.shape, 0)
            theirs = lane_ids(product.shape) % V
            shares += jnp.where(mine == theirs, product, 0.0).sum(axis=0)
        group = lane_ids(shares.shape) // V
        kept = jnp.zeros((K, 128), F32)
        for j in range(HALF):
            column = jnp.where(group == j, shares, 0.0).sum(axis=1, keepdims=True)
            for v in range(2):
                vectors = trial_ref[v]
                other = own_rows(core, vectors)[j : j + 1] * gap_ref[HALF * v : HALF * v + 1]
                column += (vectors * other).sum(axis=1, keepdims=True)
            high = column.astype(BF16).astype(F32)
            kept = jnp.where(lanes % 32 == j, high, kept)
            kept = jnp.where(lanes % 32 == HALF + j, column - high, kept)
        projection = jnp.zeros((K, 128), F32)
        for device in range(PAIRS):
            projection += arrived_ref[device, :, 2 * CB :].astype(F32)
        quarter = (TR * aux + tr) % 4
        extra = jnp.where(lanes // 32 == quarter, projection, kept)
    else:
        extra = jnp.zeros((K, 128), F32)
        for a in range(AUX):
            extra += arrived_ref[a, :, CB:].astype(F32)
    extra = extra.astype(BF16)
    for a in range(AUX):
        for t in range(TR):
            out_ref[2 * a + t, :, :CB] = owned[8 * a : 8 * a + 8, CB * t : CB * t + CB].astype(BF16)
            out_ref[2 * a + t, :, CB:] = extra


def direct_sum(arrived_ref):
    total = jnp.zeros((2 * HALF, CB), F32)
    for device in range(PAIRS):
        total += arrived_ref[device, :, :CB].astype(F32)
    return total


def middle_kernel(
    arrived_ref, pair_ref, trial_ref, gap_ref, out_ref, correction_ref, meet_ref
):
    core = lax.axis_index("grp")
    direct = direct_sum(arrived_ref)
    lanes = lane_ids((K, 128))
    tiles = []
    sums = [jnp.zeros((K, 128), F32) for _ in range(4)]
    for tile in range(TILES):
        whole = jnp.zeros((K, 128), F32)
        for quarter in range(4):
            extra = arrived_ref[4 * tile + quarter, :, CB:].astype(F32)
            whole = jnp.where(lanes // 32 == quarter, extra, whole)
            sums[quarter] += extra
        tiles.append(whole.astype(BF16))
    projection = jnp.concatenate(tiles, axis=1)
    exchange_full = lax.dot_general(projection, pair_ref[...], NT, preferred_element_type=F32)
    mine = own_rows(core, exchange_full)
    exchange = jnp.concatenate([mine[:, :CB], mine[:, CB:]], axis=0)
    shares = jnp.zeros((K, 128), F32)
    for quarter in range(4):
        shares += jnp.where(lanes // 32 == (quarter + 1) % 4, sums[quarter], 0.0)
    meet_exchange = lax.dot_general(projection, projection, NT, preferred_element_type=F32)
    meet = []
    for j in range(HALF):
        column = jnp.where(lanes % 32 % HALF == j, jnp.where(lanes % 32 < K, shares, 0.0), 0.0)
        column = column.sum(axis=1, keepdims=True)
        own = jnp.where(core == 0, meet_exchange[:, j : j + 1], meet_exchange[:, HALF + j : HALF + j + 1])
        meet.append((column + own) / (V * C))
    kept = jnp.zeros((K, 128), F32)
    for j in range(HALF):
        kept = jnp.where(lanes == j, meet[j], kept)
    meet_ref[...] = kept
    gap = gap_ref[...]
    vectors = [trial_ref[v] for v in range(2)]
    trial = jnp.concatenate([own_rows(core, vectors[v]) for v in range(2)], axis=0)
    applied = gap * trial + direct + exchange
    overlap = jnp.concatenate(
        [(vectors[v] * meet[j]).sum(axis=0, keepdims=True) for v in range(2) for j in range(HALF)],
        axis=0,
    )
    correction = (applied - overlap) / gap
    correction_ref[...] = correction
    rounded = correction.astype(BF16)
    wide = jnp.concatenate([correction[:HALF], correction[HALF:]], axis=1)
    wide = jnp.concatenate([wide, jnp.zeros_like(wide)], axis=0).astype(BF16)
    projection = dot(wide, pair_ref[...]).astype(BF16)
    for a in range(AUX):
        tile = a // 2
        out_ref[a, :, :CB] = rounded
        out_ref[a, :, CB:] = projection[:, 128 * tile : 128 * tile + 128]


def last_kernel(arrived_ref, pair_ref, correction_ref, gap_ref, out_ref):
    direct = direct_sum(arrived_ref)
    tiles = []
    for tile in range(TILES):
        whole = arrived_ref[4 * tile, :, CB:].astype(F32) + arrived_ref[4 * tile + 1, :, CB:].astype(F32)
        tiles.append(whole.astype(BF16))
    projection = jnp.concatenate(tiles, axis=1)
    exchange = lax.dot_general(projection, pair_ref[...], NT, preferred_element_type=F32)
    exchange = jnp.concatenate([exchange[:HALF, :CB], exchange[:HALF, CB:]], axis=0)
    out_ref[...] = gap_ref[...] * correction_ref[...] + direct + exchange


def direct_call(first, live, arrived, occ, virt, *local):
    out = jax.ShapeDtypeStruct((PAIRS, 2 * HALF, CB + 128), BF16)
    scratch = [
        pltpu.VMEM((HALF * V, CB), BF16),
        pltpu.VMEM((2, HALF * V, BLOCK * CB), BF16),
        pltpu.VMEM((HALF * V, C), F32),
    ]
    if first:
        scratch = [pltpu.VMEM((TR, K * V, CB), BF16), *scratch]
    return pl.pallas_call(
        functools.partial(direct_kernel, first),
        in_specs=[SMEM] + [VMEM] * (5 if first else 3),
        out_specs=VMEM,
        out_shape=out,
        scratch_shapes=scratch,
        compiler_params=params(12),
    )(live, arrived, occ, virt, *local)


def body(trial_vectors, energy_val, energy_cond, coef_occ, coef_virt, pair_coef, live_aux):
    pair = pair_coef.reshape(2 * CB, NAUX)
    virt = coef_virt.reshape(SLOTS * CB, C)
    cond = energy_cond.reshape(1, CB)

    def exchange(x, axes):
        return lax.all_to_all(x, axes, split_axis=0, concat_axis=0, tiled=True)

    sent, trial, gap, pair = pl.pallas_call(
        first_kernel,
        in_specs=[SMEM] + [HBM] * 4,
        out_specs=[VMEM] * 4,
        out_shape=[
            jax.ShapeDtypeStruct((PAIRS, K, 2 * CB + 128), BF16),
            jax.ShapeDtypeStruct((2, K, CB), F32),
            jax.ShapeDtypeStruct((2 * HALF, CB), F32),
            jax.typeof(pair),
        ],
        scratch_shapes=[
            pltpu.VMEM((1, CB), F32),
            pltpu.SMEM((2,), F32),
            pltpu.SemaphoreType.DMA((3 + PARTS,)),
        ],
        cost_estimate=pl.CostEstimate(flops=UNTIL_DIRECT, bytes_accessed=2 * pair.size, transcendentals=0),
        compiler_params=params(8),
    )(live_aux, *(stays(x) for x in (trial_vectors, pair, cond, energy_val)))
    arrived = exchange(sent, ("aux", "tr"))
    sent = direct_call(True, live_aux, arrived, coef_occ, virt, trial, gap)
    arrived = exchange(sent, ("aux", "tr"))
    sent, correction, meet = pl.pallas_call(
        middle_kernel,
        in_specs=[VMEM] * 4,
        out_specs=[VMEM] * 3,
        out_shape=[
            jax.ShapeDtypeStruct((AUX, 2 * HALF, CB + 128), BF16),
            jax.ShapeDtypeStruct((2 * HALF, CB), F32),
            jax.ShapeDtypeStruct((K, 128), F32),
        ],
        compiler_params=params(8),
    )(arrived, pair, trial, gap)
    arrived = exchange(sent, ("aux",))
    sent = direct_call(False, live_aux, arrived, coef_occ, virt)
    arrived = exchange(sent, ("aux", "tr"))
    applied = pl.pallas_call(
        last_kernel,
        in_specs=[VMEM] * 4,
        out_specs=VMEM,
        out_shape=jax.ShapeDtypeStruct((2 * HALF, CB), F32),
        compiler_params=params(8),
    )(arrived, pair, correction, gap)
    both = lax.all_gather(jnp.concatenate([applied, meet], axis=1), "grp")
    applied = both[:, :, :CB].reshape(2, 2, HALF, CB).transpose(1, 0, 2, 3).reshape(2, K, CB)
    intersection = jnp.concatenate([both[0, :, CB : CB + HALF], both[1, :, CB : CB + HALF]], axis=1)
    return (applied, intersection)


def solution(mesh):
    in_specs = (
        P("aux", None, "tr"),
        P("aux"),
        P("tr"),
        P("aux", None, None),
        P("aux", "tr", None),
        P("aux", "tr", None),
        P("aux"),
    )
    out_specs = (P("aux", None, "tr"), P())
    return jax.shard_map(body, mesh=mesh, in_specs=in_specs, out_specs=out_specs, check_vma=False)
```

```python
import functools

import jax
import jax.numpy as jnp
from jax import lax
from jax.experimental import pallas as pl
from jax.experimental.pallas import tpu as pltpu
from jax.sharding import Mesh
from jax.sharding import PartitionSpec as P

V = 64
C = 512
K = 8
SPLIT = 3
SEATS = 5
HALF = 4
AUX = 32
TR = 2
CB = C // TR
PAIRS = AUX * TR
ALL = ("zh", "tr", "y", "x")
SAME_TR = ("zh", "y", "x")
SLOTS = 64
NAUX = 2048
BLOCK = 8
STEPS = SLOTS // BLOCK
PARTS = 4
UNTIL_DIRECT = 2 * 10**10
TILES = NAUX // 128
F32 = jnp.float32
BF16 = jnp.bfloat16
VMEM = pl.BlockSpec(memory_space=pltpu.VMEM)
SMEM = pl.BlockSpec(memory_space=pltpu.SMEM)
HBM = pl.BlockSpec(memory_space=pltpu.HBM)
NT = (((1,), (1,)), ((), ()))


def place(a, t):
    y, zh, x = a // 8, a // 4 % 2, a % 4
    return zh * 32 + t * 16 + y * 4 + x


def place_same_tr(a):
    y, zh, x = a // 8, a // 4 % 2, a % 4
    return zh * 16 + y * 4 + x


def stays(x):
    return pltpu.with_memory_space_constraint(x, pltpu.HBM)


def params(mib):
    return pltpu.CompilerParams(vmem_limit_bytes=mib * 2**20)


def dot(a, b):
    return jnp.dot(a, b, preferred_element_type=F32)


def lane_ids(shape):
    return lax.broadcasted_iota(jnp.int32, shape, len(shape) - 1)


def row_ids(shape):
    return lax.broadcasted_iota(jnp.int32, shape, 0)


def own_seats(core, rows):
    return jnp.where(core == 0, rows[:SEATS], rows[K - SEATS :])


def both_halves(rows):
    return jnp.concatenate([rows[:, :CB], rows[:, CB:]], axis=0)


def first_kernel(
    live_ref, trial_hbm, pair_hbm, cond_hbm, val_hbm, out_ref, trial_ref, gap_ref, pair_ref, cond_ref, val_ref, sems
):
    parts = [pl.ds(NAUX // PARTS * i, NAUX // PARTS) for i in range(PARTS)]
    copies = [
        pltpu.make_async_copy(trial_hbm, trial_ref, sems.at[0]),
        pltpu.make_async_copy(cond_hbm, cond_ref, sems.at[1]),
        pltpu.make_async_copy(val_hbm, val_ref, sems.at[2]),
    ]
    for i in range(PARTS):
        copies.append(pltpu.make_async_copy(pair_hbm.at[:, parts[i]], pair_ref.at[:, parts[i]], sems.at[3 + i]))
    for copy in copies:
        copy.start()
    copies[0].wait()
    wide = jnp.concatenate([trial_ref[v].astype(BF16) for v in range(2)], axis=1)
    for device in range(PAIRS):
        out_ref[device, :, : 2 * CB] = wide
    copies[1].wait()
    copies[2].wait()
    for v in range(2):
        gap_ref[HALF * v : HALF * v + HALF] = jnp.broadcast_to(cond_ref[...] - val_ref[v], (HALF, CB))
    for i in range(PARTS):
        copies[3 + i].wait()
        projection = dot(wide, pair_ref[:, parts[i]]).astype(BF16)
        for tile in range(TILES // PARTS):
            for device in range(4):
                at = 4 * (TILES // PARTS * i + tile) + device
                out_ref[at, :, 2 * CB :] = projection[:, 128 * tile : 128 * tile + 128]


def direct_kernel(first, *refs):
    if first:
        live_ref, arrived_ref, occ_ref, virt_ref, trial_ref, gap_ref, out_ref = refs[:7]
        rows_ref, vectors_ref, blended_ref, total_ref = refs[7:]
    else:
        live_ref, arrived_ref, occ_ref, virt_ref, out_ref = refs[:5]
        vectors_ref, blended_ref, total_ref = refs[5:]
    core, tr, quarter = lax.axis_index("grp"), lax.axis_index("tr"), lax.axis_index("x")

    if first:
        for a in range(AUX):
            for t in range(TR):
                slab = arrived_ref[place(a, t), :, : 2 * CB].astype(F32)
                rows_ref[t, 16 * a : 16 * a + 16] = both_halves(slab).astype(BF16)
        row = row_ids((SEATS * V, 1))
        wanted = K * (row % V) + SPLIT * core + row // V
        chosen = lane_ids((SEATS * V, K * V)) == wanted
        vectors_ref[...] = dot(chosen.astype(BF16), rows_ref[tr]).astype(BF16)
    else:
        tiles = [arrived_ref[place_same_tr(a)].astype(F32) for a in range(AUX)]
        wide = jnp.concatenate(tiles, axis=0).astype(BF16)
        row = row_ids((HALF * V, 1))
        chosen = lane_ids((HALF * V, 8 * AUX)) == HALF * (row % V) + row // V
        vectors_ref[: HALF * V] = dot(chosen.astype(BF16), wide[:, :CB]).astype(BF16)
        row = row_ids((V, 1))
        for h in range(2):
            chosen = lane_ids((V, 8 * AUX)) == 8 * (row // 2) + 2 * h + row % 2
            part = dot(chosen.astype(BF16), wide[:, CB:]).astype(BF16)
            vectors_ref[HALF * V :, 128 * h : 128 * h + 128] = part

    live = live_ref[0]

    def accumulate(seats):
        slot = row_ids((BLOCK * V, V)) // V
        size = seats * V

        def blend(step):
            occ = occ_ref[BLOCK * step : BLOCK * step + BLOCK].reshape(BLOCK * V, V)
            occ = jnp.where(slot < live - step * BLOCK, occ, jnp.zeros_like(occ))
            for k in range(seats):
                piece = dot(occ, vectors_ref[V * k : V * k + V]).astype(BF16)
                for p in range(BLOCK):
                    blended_ref[step % 2, V * k : V * k + V, CB * p : CB * p + CB] = piece[V * p : V * p + V]

        blend(0)
        for step in range(STEPS):
            rows = slice(step * BLOCK * CB, (step + 1) * BLOCK * CB)
            product = dot(blended_ref[step % 2, :size], virt_ref[rows])
            if step + 1 < STEPS:
                blend(step + 1)
            if step == 0:
                total_ref[:size] = product
            else:
                total_ref[:size] += product
        if seats < SEATS:
            total_ref[size:] = jnp.zeros((SEATS * V - size, C), F32)

    @pl.when(core == 0)
    def _():
        accumulate(SPLIT)

    @pl.when(core != 0)
    def _():
        accumulate(SEATS)

    total = total_ref[...].astype(BF16)
    row = row_ids((HALF * V, 1))
    chosen = lane_ids((HALF * V, HALF * V)) == V * (row % HALF) + row // HALF
    owned = dot(chosen.astype(BF16), total[: HALF * V]).astype(BF16).astype(F32)
    late = [
        jnp.concatenate([total[HALF * V :, CB * t + 128 * h : CB * t + 128 * h + 128] for t in range(TR)], axis=1)
        for h in range(2)
    ]
    row = row_ids((8 * AUX, 1))
    chosen = lane_ids((8 * AUX, 2 * V)) == V * (row % 8 // 2) + 2 * (row // 8) + row % 2
    chosen = jnp.where(row % 8 < 4, chosen.astype(F32), 0.0)
    late = dot(chosen.astype(BF16), jnp.concatenate(late, axis=0))

    lanes = lane_ids((K, 128))
    if first:
        shares = jnp.zeros((K, SEATS * V), F32)
        for t in range(TR):
            product = lax.dot_general(
                rows_ref[t], total[:, CB * t : CB * t + CB], NT, preferred_element_type=F32
            ).reshape(V, K, SEATS * V)
            theirs = lane_ids(product.shape) % V
            shares += jnp.where(row_ids(product.shape) == theirs, product, 0.0).sum(axis=0)
        group = lane_ids(shares.shape) // V
        kept = jnp.zeros((K, 128), F32)
        for j in range(SEATS):
            column = jnp.where(group == j, shares, 0.0).sum(axis=1, keepdims=True)
            for v in range(2):
                vectors = trial_ref[v]
                other = own_seats(core, vectors)[j : j + 1] * gap_ref[HALF * v : HALF * v + 1]
                column += (vectors * other).sum(axis=1, keepdims=True)
            high = column.astype(BF16).astype(F32)
            kept = jnp.where(lanes % 32 == j, high, kept)
            kept = jnp.where(lanes % 32 == 8 + j, column - high, kept)
        projection = jnp.zeros((K, 128), F32)
        for device in range(PAIRS):
            projection += arrived_ref[device, :, 2 * CB :].astype(F32)
        extra = jnp.where(lanes // 32 == quarter, projection, kept)
        near = lax.rem(lanes // 32 - quarter + 4, 4) < 2
        extra = jnp.where(near, pltpu.roll(extra, 4, 0), pltpu.roll(extra, 64, 1))
    else:
        extra = jnp.zeros((K, 128), F32)
        for tile in tiles:
            extra += tile[:, CB:]
    extra = jnp.where(row_ids((K, 128)) >= 4, extra, 0.0)
    for a in range(AUX):
        for t in range(TR):
            out_ref[place(a, t), :, :CB] = owned[8 * a : 8 * a + 8, CB * t : CB * t + CB].astype(BF16)
            part = late[8 * a : 8 * a + 8, 128 * t : 128 * t + 128] + extra
            out_ref[place(a, t), :, CB:] = part.astype(BF16)


def direct_sum(arrived_ref):
    total = jnp.zeros((8, CB + 128), F32)
    for device in range(PAIRS):
        total += arrived_ref[device].astype(F32)
    return total[:, :CB], jnp.concatenate([total[:2, CB:], total[2:4, CB:]], axis=1)


def seat_rows(own):
    rows = jnp.concatenate([own[:HALF, :CB], own[:HALF, CB:]], axis=0)
    return rows, jnp.concatenate([own[HALF:SEATS, :CB], own[HALF:SEATS, CB:]], axis=0)


def middle_kernel(
    arrived_ref, pair_ref, trial_ref, gap_ref, out_ref, correction_ref, meet_ref
):
    core = lax.axis_index("grp")
    direct = direct_sum(arrived_ref)
    lanes, rows = lane_ids((K, 128)), row_ids((K, 128))
    tiles = []
    sums = [jnp.zeros((K, 128), F32) for _ in range(4)]
    for tile in range(TILES):
        low = high = jnp.zeros((K, 128), F32)
        for quarter in range(4):
            extra = arrived_ref[4 * tile + quarter, :, CB:].astype(F32)
            low = jnp.where(lanes // 32 == quarter, extra, low)
            high = jnp.where(lanes // 32 == (quarter + 2) % 4, extra, high)
            sums[quarter] += extra
        whole = jnp.where(rows < 4, pltpu.roll(low, 4, 0), pltpu.roll(high, 64, 1))
        tiles.append(whole.astype(BF16))
    projection = jnp.concatenate(tiles, axis=1)
    exchange = lax.dot_general(projection, pair_ref[...], NT, preferred_element_type=F32)
    exchange = seat_rows(own_seats(core, exchange))
    low = high = jnp.zeros((K, 128), F32)
    for quarter in range(4):
        low = jnp.where(lanes // 32 == (quarter + 1) % 4, sums[quarter], low)
        high = jnp.where(lanes // 32 == (quarter + 3) % 4, sums[quarter], high)
    shares = jnp.where(rows < 4, pltpu.roll(low, 4, 0), high)
    meet_exchange = lax.dot_general(projection, projection, NT, preferred_element_type=F32)
    meet = []
    kept = jnp.zeros((K, 128), F32)
    for j in range(SEATS):
        mine = (lanes % 32 == j) | (lanes % 32 == 8 + j)
        column = jnp.where(mine, shares, 0.0).sum(axis=1, keepdims=True)
        other = K - SEATS + j
        column += jnp.where(core == 0, meet_exchange[:, j : j + 1], meet_exchange[:, other : other + 1])
        meet.append(column / (V * C))
        kept = jnp.where(lanes == j, meet[j], kept)
    meet_ref[...] = kept
    vectors = [trial_ref[v] for v in range(2)]
    trial = seat_rows(jnp.concatenate([own_seats(core, vectors[v]) for v in range(2)], axis=1))
    gaps = (gap_ref[...], jnp.concatenate([gap_ref[:1], gap_ref[HALF : HALF + 1]], axis=0))
    seats = (range(HALF), range(HALF, SEATS))
    correction = []
    for i in range(2):
        applied = gaps[i] * trial[i] + direct[i] + exchange[i]
        overlap = [(vectors[v] * meet[j]).sum(axis=0, keepdims=True) for v in range(2) for j in seats[i]]
        correction.append((applied - jnp.concatenate(overlap, axis=0)) / gaps[i])
    rows4, rows1 = correction
    correction_ref[:8] = rows4
    correction_ref[8:] = jnp.concatenate([rows1, jnp.zeros((6, CB), F32)], axis=0)
    wide = jnp.concatenate(
        [
            jnp.concatenate([rows4[:HALF], rows4[HALF:]], axis=1),
            jnp.concatenate([rows1[:1], rows1[1:]], axis=1),
            jnp.zeros((K - SEATS, 2 * CB), F32),
        ],
        axis=0,
    )
    projection = dot(wide.astype(BF16), pair_ref[...]).astype(BF16).astype(F32)
    rounded = rows4.astype(BF16)
    late = jnp.concatenate([rows1[:, :128], rows1[:, 128:]], axis=0)
    for tile in range(TILES):
        part = projection[:, 128 * tile : 128 * tile + 128]
        here = jnp.concatenate([late, part[:HALF]], axis=0)
        away = jnp.broadcast_to(pltpu.roll(part, 64, 1)[HALF:SEATS], (4, 128))
        away = jnp.concatenate([late, away], axis=0)
        for half in range(2):
            out_ref[2 * tile + half, :, :CB] = rounded
            both = jnp.where(lanes // 64 == half, here, away)
            out_ref[2 * tile + half, :, CB:] = both.astype(BF16)


def last_kernel(arrived_ref, pair_ref, correction_ref, gap_ref, meet_ref, out_ref):
    direct = direct_sum(arrived_ref)
    lanes, rows = lane_ids((K, 128)), row_ids((K, 128))
    tiles = []
    for tile in range(TILES):
        at = tile // 8 * 32 + 2 * tile % 16
        parts = [
            arrived_ref[at + half, :, CB:].astype(F32) + arrived_ref[at + 16 + half, :, CB:].astype(F32)
            for half in range(2)
        ]
        here = jnp.where(lanes < 64, parts[0], parts[1])
        away = pltpu.roll(jnp.where(lanes < 64, parts[1], parts[0]), 64, 1)
        tiles.append(jnp.where(rows >= 4, here, pltpu.roll(away, 4, 0)).astype(BF16))
    projection = jnp.concatenate(tiles, axis=1)
    exchange = lax.dot_general(projection, pair_ref[...], NT, preferred_element_type=F32)
    exchange = seat_rows(jnp.concatenate([exchange[HALF:], exchange[:1]], axis=0))
    out_ref[:, :CB] = gap_ref[...] * correction_ref[:8] + direct[0] + exchange[0]
    out_ref[:, CB : CB + 128] = meet_ref[...]
    gap = jnp.concatenate([gap_ref[:1], gap_ref[HALF : HALF + 1]], axis=0)
    late = gap * correction_ref[8:10] + direct[1] + exchange[1]
    out_ref[:, CB + 128 :] = jnp.concatenate([late, jnp.zeros((6, CB), F32)], axis=0)


def join_kernel(both_ref, applied_ref, meet_ref):
    for v in range(2):
        rows = [
            both_ref[0, HALF * v : HALF * v + SPLIT, :CB],
            both_ref[1, HALF * v : HALF * v + HALF, :CB],
            both_ref[1, v : v + 1, CB + 128 :],
        ]
        applied_ref[v] = jnp.concatenate(rows, axis=0)
    columns = [both_ref[0, :, CB : CB + SPLIT], both_ref[1, :, CB : CB + SEATS]]
    meet_ref[...] = jnp.concatenate(columns, axis=1)


def direct_call(first, live, arrived, occ, virt, *local):
    out = jax.ShapeDtypeStruct((PAIRS, 8, CB + 128), BF16)
    scratch = [
        pltpu.VMEM((SEATS * V, CB), BF16),
        pltpu.VMEM((2, SEATS * V, BLOCK * CB), BF16),
        pltpu.VMEM((SEATS * V, C), F32),
    ]
    if first:
        scratch = [pltpu.VMEM((TR, K * V, CB), BF16), *scratch]
    return pl.pallas_call(
        functools.partial(direct_kernel, first),
        in_specs=[SMEM] + [VMEM] * (5 if first else 3),
        out_specs=VMEM,
        out_shape=out,
        scratch_shapes=scratch,
        compiler_params=params(12),
    )(live, arrived, occ, virt, *local)


def body(trial_vectors, energy_val, energy_cond, coef_occ, coef_virt, pair_coef, live_aux):
    pair = pair_coef.reshape(2 * CB, NAUX)
    virt = coef_virt.reshape(SLOTS * CB, C)
    cond = energy_cond.reshape(1, CB)

    def exchange(x, axes):
        return lax.all_to_all(x, axes, split_axis=0, concat_axis=0, tiled=True)

    sent, trial, gap, pair = pl.pallas_call(
        first_kernel,
        in_specs=[SMEM] + [HBM] * 4,
        out_specs=[VMEM] * 4,
        out_shape=[
            jax.ShapeDtypeStruct((PAIRS, K, 2 * CB + 128), BF16),
            jax.ShapeDtypeStruct((2, K, CB), F32),
            jax.ShapeDtypeStruct((2 * HALF, CB), F32),
            jax.typeof(pair),
        ],
        scratch_shapes=[
            pltpu.VMEM((1, CB), F32),
            pltpu.SMEM((2,), F32),
            pltpu.SemaphoreType.DMA((3 + PARTS,)),
        ],
        cost_estimate=pl.CostEstimate(flops=UNTIL_DIRECT, bytes_accessed=2 * pair.size, transcendentals=0),
        compiler_params=params(8),
    )(live_aux, *(stays(x) for x in (trial_vectors, pair, cond, energy_val)))
    arrived = exchange(sent, ALL)
    sent = direct_call(True, live_aux, arrived, coef_occ, virt, trial, gap)
    arrived = exchange(sent, ALL)
    sent, correction, meet = pl.pallas_call(
        middle_kernel,
        in_specs=[VMEM] * 4,
        out_specs=[VMEM] * 3,
        out_shape=[
            jax.ShapeDtypeStruct((AUX, 8, CB + 128), BF16),
            jax.ShapeDtypeStruct((16, CB), F32),
            jax.ShapeDtypeStruct((K, 128), F32),
        ],
        compiler_params=params(8),
    )(arrived, pair, trial, gap)
    arrived = exchange(sent, SAME_TR)
    sent = direct_call(False, live_aux, arrived, coef_occ, virt)
    arrived = exchange(sent, ALL)
    mine = pl.pallas_call(
        last_kernel,
        in_specs=[VMEM] * 5,
        out_specs=VMEM,
        out_shape=jax.ShapeDtypeStruct((8, 2 * CB + 128), F32),
        compiler_params=params(8),
    )(arrived, pair, correction, gap, meet)
    both = lax.all_gather(mine, "grp")
    applied, intersection = pl.pallas_call(
        join_kernel,
        in_specs=[VMEM],
        out_specs=[VMEM] * 2,
        out_shape=[jax.ShapeDtypeStruct((2, K, CB), F32), jax.ShapeDtypeStruct((K, K), F32)],
        compiler_params=params(4),
    )(both)
    return (applied, intersection)


def solution(mesh):
    mesh = Mesh(mesh.devices.reshape(2, 4, 2, 4, TR), ("grp", "y", "zh", "x", "tr"))
    aux = ("y", "zh", "x")
    in_specs = (
        P(aux, None, "tr"),
        P(aux),
        P("tr"),
        P(aux, None, None),
        P(aux, "tr", None),
        P(aux, "tr", None),
        P(aux),
    )
    out_specs = (P(aux, None, "tr"), P())
    return jax.shard_map(body, mesh=mesh, in_specs=in_specs, out_specs=out_specs, check_vma=False)
```

```python
import functools

import jax
import jax.numpy as jnp
from jax import lax
from jax.experimental import pallas as pl
from jax.experimental.pallas import tpu as pltpu
from jax.sharding import Mesh
from jax.sharding import PartitionSpec as P

V = 64
C = 512
K = 8
HALF = 4
AUX = 32
TR = 2
CB = C // TR
PAIRS = AUX * TR
ALL = ("zh", "tr", "y", "x")
SAME_TR = ("zh", "y", "x")
SLOTS = 64
NAUX = 2048
BLOCK = 8
STEPS = SLOTS // BLOCK
PARTS = 4
UNTIL_DIRECT = 2 * 10**10
TILES = NAUX // 128
F32 = jnp.float32
BF16 = jnp.bfloat16
VMEM = pl.BlockSpec(memory_space=pltpu.VMEM)
SMEM = pl.BlockSpec(memory_space=pltpu.SMEM)
HBM = pl.BlockSpec(memory_space=pltpu.HBM)
NT = (((1,), (1,)), ((), ()))


def place(a, t):
    y, zh, x = a // 8, a // 4 % 2, a % 4
    return zh * 32 + t * 16 + y * 4 + x


def place_same_tr(a):
    y, zh, x = a // 8, a // 4 % 2, a % 4
    return zh * 16 + y * 4 + x


def stays(x):
    return pltpu.with_memory_space_constraint(x, pltpu.HBM)


def params(mib):
    return pltpu.CompilerParams(vmem_limit_bytes=mib * 2**20)


def dot(a, b):
    return jnp.dot(a, b, preferred_element_type=F32)


def lane_ids(shape):
    return lax.broadcasted_iota(jnp.int32, shape, len(shape) - 1)


def own_rows(core, rows):
    return jnp.where(core == 0, rows[:HALF], rows[HALF:])


def both_halves(rows):
    return jnp.concatenate([rows[:, :CB], rows[:, CB:]], axis=0)


def first_kernel(
    live_ref, trial_hbm, pair_hbm, cond_hbm, val_hbm, out_ref, trial_ref, gap_ref, pair_ref, cond_ref, val_ref, sems
):
    parts = [pl.ds(2 * CB // PARTS * i, 2 * CB // PARTS) for i in range(PARTS)]
    copies = [
        pltpu.make_async_copy(trial_hbm, trial_ref, sems.at[0]),
        pltpu.make_async_copy(cond_hbm, cond_ref, sems.at[1]),
        pltpu.make_async_copy(val_hbm, val_ref, sems.at[2]),
    ]
    for i in range(PARTS):
        copies.append(pltpu.make_async_copy(pair_hbm.at[parts[i]], pair_ref.at[parts[i]], sems.at[3 + i]))
    for copy in copies:
        copy.start()
    copies[0].wait()
    wide = jnp.concatenate([trial_ref[v].astype(BF16) for v in range(2)], axis=1)
    for device in range(PAIRS):
        out_ref[device, :, : 2 * CB] = wide
    copies[1].wait()
    copies[2].wait()
    for v in range(2):
        gap_ref[HALF * v : HALF * v + HALF] = jnp.broadcast_to(cond_ref[...] - val_ref[v], (HALF, CB))
    projection = jnp.zeros((K, NAUX), F32)
    for i in range(PARTS):
        copies[3 + i].wait()
        rows = slice(2 * CB // PARTS * i, 2 * CB // PARTS * (i + 1))
        projection += dot(wide[:, rows], pair_ref[rows])
    projection = projection.astype(BF16)
    for device in range(PAIRS):
        tile = device // 4
        out_ref[device, :, 2 * CB :] = projection[:, 128 * tile : 128 * tile + 128]


def direct_kernel(first, *refs):
    if first:
        live_ref, arrived_ref, occ_ref, virt_ref, trial_ref, gap_ref = refs[:6]
        out_ref, rows_ref, vectors_ref, blended_ref, total_ref = refs[6:]
    else:
        live_ref, arrived_ref, occ_ref, virt_ref = refs[:4]
        out_ref, vectors_ref, blended_ref, total_ref = refs[4:]
    core, tr, quarter = lax.axis_index("grp"), lax.axis_index("tr"), lax.axis_index("x")

    row = lax.broadcasted_iota(jnp.int32, (HALF * V, 1), 0)
    if first:
        for a in range(AUX):
            for t in range(TR):
                slab = arrived_ref[place(a, t), :, : 2 * CB].astype(F32)
                rows_ref[t, 16 * a : 16 * a + 16] = both_halves(slab).astype(BF16)
        chosen = lax.broadcasted_iota(jnp.int32, (HALF * V, K * V), 1)
        wanted = K * (row % V) + HALF * core + row // V
        wide = rows_ref[tr]
    else:
        chosen = lax.broadcasted_iota(jnp.int32, (HALF * V, HALF * V), 1)
        wanted = HALF * (row % V) + row // V
        wide = [arrived_ref[place_same_tr(a), :, :CB].astype(F32) for a in range(AUX)]
        wide = jnp.concatenate(wide, axis=0).astype(BF16)
    vectors_ref[...] = dot((chosen == wanted).astype(BF16), wide).astype(BF16)

    live = live_ref[0]
    slot = lax.broadcasted_iota(jnp.int32, (BLOCK * V, V), 0) // V

    def blend(step):
        occ = occ_ref[BLOCK * step : BLOCK * step + BLOCK].reshape(BLOCK * V, V)
        occ = jnp.where(slot < live - step * BLOCK, occ, jnp.zeros_like(occ))
        for k in range(HALF):
            piece = dot(occ, vectors_ref[V * k : V * k + V]).astype(BF16)
            for p in range(BLOCK):
                blended_ref[step % 2, V * k : V * k + V, CB * p : CB * p + CB] = piece[V * p : V * p + V]

    blend(0)
    for step in range(STEPS):
        rows = slice(step * BLOCK * CB, (step + 1) * BLOCK * CB)
        product = dot(blended_ref[step % 2], virt_ref[rows])
        if step + 1 < STEPS:
            blend(step + 1)
        if step == 0:
            total_ref[...] = product
        else:
            total_ref[...] += product

    lanes = lane_ids((K, 128))
    total = total_ref[...].astype(BF16)
    chosen = lax.broadcasted_iota(jnp.int32, (HALF * V, HALF * V), 1)
    owned = dot((chosen == V * (row % HALF) + row // HALF).astype(BF16), total).astype(BF16).astype(F32)
    if first:
        shares = jnp.zeros((K, HALF * V), F32)
        for t in range(TR):
            product = lax.dot_general(
                rows_ref[t], total[:, CB * t : CB * t + CB], NT, preferred_element_type=F32
            ).reshape(V, K, HALF * V)
            mine = lax.broadcasted_iota(jnp.int32, product.shape, 0)
            theirs = lane_ids(product.shape) % V
            shares += jnp.where(mine == theirs, product, 0.0).sum(axis=0)
        group = lane_ids(shares.shape) // V
        kept = jnp.zeros((K, 128), F32)
        for j in range(HALF):
            column = jnp.where(group == j, shares, 0.0).sum(axis=1, keepdims=True)
            for v in range(2):
                vectors = trial_ref[v]
                other = own_rows(core, vectors)[j : j + 1] * gap_ref[HALF * v : HALF * v + 1]
                column += (vectors * other).sum(axis=1, keepdims=True)
            high = column.astype(BF16).astype(F32)
            kept = jnp.where(lanes % 32 == j, high, kept)
            kept = jnp.where(lanes % 32 == HALF + j, column - high, kept)
        projection = jnp.zeros((K, 128), F32)
        for device in range(PAIRS):
            projection += arrived_ref[device, :, 2 * CB :].astype(F32)
        extra = jnp.where(lanes // 32 == quarter, projection, kept)
    else:
        extra = jnp.zeros((K, 128), F32)
        for a in range(AUX):
            extra += arrived_ref[a, :, CB:].astype(F32)
    extra = extra.astype(BF16)
    for a in range(AUX):
        for t in range(TR):
            out_ref[place(a, t), :, :CB] = owned[8 * a : 8 * a + 8, CB * t : CB * t + CB].astype(BF16)
            out_ref[place(a, t), :, CB:] = extra


def direct_sum(arrived_ref):
    total = jnp.zeros((2 * HALF, CB), F32)
    for device in range(PAIRS):
        total += arrived_ref[device, :, :CB].astype(F32)
    return total


def middle_kernel(
    arrived_ref, pair_ref, trial_ref, gap_ref, out_ref, correction_ref, meet_ref
):
    core = lax.axis_index("grp")
    direct = direct_sum(arrived_ref)
    lanes = lane_ids((K, 128))
    tiles = []
    sums = [jnp.zeros((K, 128), F32) for _ in range(4)]
    for tile in range(TILES):
        whole = jnp.zeros((K, 128), F32)
        for quarter in range(4):
            extra = arrived_ref[4 * tile + quarter, :, CB:].astype(F32)
            whole = jnp.where(lanes // 32 == quarter, extra, whole)
            sums[quarter] += extra
        tiles.append(whole.astype(BF16))
    projection = jnp.concatenate(tiles, axis=1)
    exchange_full = lax.dot_general(projection, pair_ref[...], NT, preferred_element_type=F32)
    mine = own_rows(core, exchange_full)
    exchange = jnp.concatenate([mine[:, :CB], mine[:, CB:]], axis=0)
    shares = jnp.zeros((K, 128), F32)
    for quarter in range(4):
        shares += jnp.where(lanes // 32 == (quarter + 1) % 4, sums[quarter], 0.0)
    meet_exchange = lax.dot_general(projection, projection, NT, preferred_element_type=F32)
    meet = []
    for j in range(HALF):
        column = jnp.where(lanes % 32 % HALF == j, jnp.where(lanes % 32 < K, shares, 0.0), 0.0)
        column = column.sum(axis=1, keepdims=True)
        own = jnp.where(core == 0, meet_exchange[:, j : j + 1], meet_exchange[:, HALF + j : HALF + j + 1])
        meet.append((column + own) / (V * C))
    kept = jnp.zeros((K, 128), F32)
    for j in range(HALF):
        kept = jnp.where(lanes == j, meet[j], kept)
    meet_ref[...] = kept
    gap = gap_ref[...]
    vectors = [trial_ref[v] for v in range(2)]
    trial = jnp.concatenate([own_rows(core, vectors[v]) for v in range(2)], axis=0)
    applied = gap * trial + direct + exchange
    overlap = jnp.concatenate(
        [(vectors[v] * meet[j]).sum(axis=0, keepdims=True) for v in range(2) for j in range(HALF)],
        axis=0,
    )
    correction = (applied - overlap) / gap
    correction_ref[...] = correction
    rounded = correction.astype(BF16)
    wide = jnp.concatenate([correction[:HALF], correction[HALF:]], axis=1)
    wide = jnp.concatenate([wide, jnp.zeros_like(wide)], axis=0).astype(BF16)
    projection = dot(wide, pair_ref[...]).astype(BF16)
    for a in range(AUX):
        tile = a // 2
        out_ref[a, :, :CB] = rounded
        out_ref[a, :, CB:] = projection[:, 128 * tile : 128 * tile + 128]


def last_kernel(arrived_ref, pair_ref, correction_ref, gap_ref, meet_ref, out_ref):
    direct = direct_sum(arrived_ref)
    tiles = []
    for tile in range(TILES):
        at = tile // 8 * 32 + 2 * tile % 16
        whole = arrived_ref[at, :, CB:].astype(F32) + arrived_ref[at + 16, :, CB:].astype(F32)
        tiles.append(whole.astype(BF16))
    projection = jnp.concatenate(tiles, axis=1)
    exchange = lax.dot_general(projection, pair_ref[...], NT, preferred_element_type=F32)
    exchange = jnp.concatenate([exchange[:HALF, :CB], exchange[:HALF, CB:]], axis=0)
    out_ref[:, :CB] = gap_ref[...] * correction_ref[...] + direct + exchange
    out_ref[:, CB:] = meet_ref[...]


def join_kernel(both_ref, applied_ref, meet_ref):
    for v in range(2):
        rows = [both_ref[core, HALF * v : HALF * v + HALF, :CB] for core in range(2)]
        applied_ref[v] = jnp.concatenate(rows, axis=0)
    columns = [both_ref[core, :, CB : CB + HALF] for core in range(2)]
    meet_ref[...] = jnp.concatenate(columns, axis=1)


def direct_call(first, live, arrived, occ, virt, *local):
    out = jax.ShapeDtypeStruct((PAIRS, 2 * HALF, CB + 128), BF16)
    scratch = [
        pltpu.VMEM((HALF * V, CB), BF16),
        pltpu.VMEM((2, HALF * V, BLOCK * CB), BF16),
        pltpu.VMEM((HALF * V, C), F32),
    ]
    if first:
        scratch = [pltpu.VMEM((TR, K * V, CB), BF16), *scratch]
    return pl.pallas_call(
        functools.partial(direct_kernel, first),
        in_specs=[SMEM] + [VMEM] * (5 if first else 3),
        out_specs=VMEM,
        out_shape=out,
        scratch_shapes=scratch,
        compiler_params=params(12),
    )(live, arrived, occ, virt, *local)


def body(trial_vectors, energy_val, energy_cond, coef_occ, coef_virt, pair_coef, live_aux):
    pair = pair_coef.reshape(2 * CB, NAUX)
    virt = coef_virt.reshape(SLOTS * CB, C)
    cond = energy_cond.reshape(1, CB)

    def exchange(x, axes):
        return lax.all_to_all(x, axes, split_axis=0, concat_axis=0, tiled=True)

    sent, trial, gap, pair = pl.pallas_call(
        first_kernel,
        in_specs=[SMEM] + [HBM] * 4,
        out_specs=[VMEM] * 4,
        out_shape=[
            jax.ShapeDtypeStruct((PAIRS, K, 2 * CB + 128), BF16),
            jax.ShapeDtypeStruct((2, K, CB), F32),
            jax.ShapeDtypeStruct((2 * HALF, CB), F32),
            jax.typeof(pair),
        ],
        scratch_shapes=[
            pltpu.VMEM((1, CB), F32),
            pltpu.SMEM((2,), F32),
            pltpu.SemaphoreType.DMA((3 + PARTS,)),
        ],
        cost_estimate=pl.CostEstimate(flops=UNTIL_DIRECT, bytes_accessed=2 * pair.size, transcendentals=0),
        compiler_params=params(8),
    )(live_aux, *(stays(x) for x in (trial_vectors, pair, cond, energy_val)))
    arrived = exchange(sent, ALL)
    sent = direct_call(True, live_aux, arrived, coef_occ, virt, trial, gap)
    arrived = exchange(sent, ALL)
    sent, correction, meet = pl.pallas_call(
        middle_kernel,
        in_specs=[VMEM] * 4,
        out_specs=[VMEM] * 3,
        out_shape=[
            jax.ShapeDtypeStruct((AUX, 2 * HALF, CB + 128), BF16),
            jax.ShapeDtypeStruct((2 * HALF, CB), F32),
            jax.ShapeDtypeStruct((K, 128), F32),
        ],
        compiler_params=params(8),
    )(arrived, pair, trial, gap)
    arrived = exchange(sent, SAME_TR)
    sent = direct_call(False, live_aux, arrived, coef_occ, virt)
    arrived = exchange(sent, ALL)
    mine = pl.pallas_call(
        last_kernel,
        in_specs=[VMEM] * 5,
        out_specs=VMEM,
        out_shape=jax.ShapeDtypeStruct((2 * HALF, CB + 128), F32),
        compiler_params=params(8),
    )(arrived, pair, correction, gap, meet)
    both = lax.all_gather(mine, "grp")
    applied, intersection = pl.pallas_call(
        join_kernel,
        in_specs=[VMEM],
        out_specs=[VMEM] * 2,
        out_shape=[jax.ShapeDtypeStruct((2, K, CB), F32), jax.ShapeDtypeStruct((K, K), F32)],
        compiler_params=params(4),
    )(both)
    return (applied, intersection)


def solution(mesh):
    mesh = Mesh(mesh.devices.reshape(2, 4, 2, 4, TR), ("grp", "y", "zh", "x", "tr"))
    aux = ("y", "zh", "x")
    in_specs = (
        P(aux, None, "tr"),
        P(aux),
        P("tr"),
        P(aux, None, None),
        P(aux, "tr", None),
        P(aux, "tr", None),
        P(aux),
    )
    out_specs = (P(aux, None, "tr"), P())
    return jax.shard_map(body, mesh=mesh, in_specs=in_specs, out_specs=out_specs, check_vma=False)
```

```python
import functools

import jax
import jax.numpy as jnp
from jax import lax
from jax.experimental import pallas as pl
from jax.experimental.pallas import tpu as pltpu
from jax.sharding import Mesh
from jax.sharding import PartitionSpec as P

V = 64
C = 512
K = 8
HALF = 4
AUX = 32
TR = 2
CB = C // TR
PAIRS = AUX * TR
ALL = ("zh", "tr", "y", "x")
SAME_TR = ("zh", "y", "x")
SLOTS = 64
NAUX = 2048
BLOCK = 8
STEPS = SLOTS // BLOCK
PARTS = 4
UNTIL_DIRECT = 2 * 10**10
TILES = NAUX // 128
F32 = jnp.float32
BF16 = jnp.bfloat16
VMEM = pl.BlockSpec(memory_space=pltpu.VMEM)
SMEM = pl.BlockSpec(memory_space=pltpu.SMEM)
HBM = pl.BlockSpec(memory_space=pltpu.HBM)
NT = (((1,), (1,)), ((), ()))


def place(a, t):
    y, zh, x = a // 8, a // 4 % 2, a % 4
    return zh * 32 + t * 16 + y * 4 + x


def place_same_tr(a):
    y, zh, x = a // 8, a // 4 % 2, a % 4
    return zh * 16 + y * 4 + x


def stays(x):
    return pltpu.with_memory_space_constraint(x, pltpu.HBM)


def params(mib):
    return pltpu.CompilerParams(vmem_limit_bytes=mib * 2**20)


def dot(a, b):
    return jnp.dot(a, b, preferred_element_type=F32)


def lane_ids(shape):
    return lax.broadcasted_iota(jnp.int32, shape, len(shape) - 1)


def own_rows(core, rows):
    return jnp.where(core == 0, rows[:HALF], rows[HALF:])


def both_halves(rows):
    return jnp.concatenate([rows[:, :CB], rows[:, CB:]], axis=0)


def first_kernel(
    live_ref, trial_hbm, pair_hbm, cond_hbm, val_hbm, out_ref, trial_ref, gap_ref, pair_ref, cond_ref, val_ref, sems
):
    parts = [pl.ds(2 * CB // PARTS * i, 2 * CB // PARTS) for i in range(PARTS)]
    copies = [
        pltpu.make_async_copy(trial_hbm, trial_ref, sems.at[0]),
        pltpu.make_async_copy(cond_hbm, cond_ref, sems.at[1]),
        pltpu.make_async_copy(val_hbm, val_ref, sems.at[2]),
    ]
    for i in range(PARTS):
        copies.append(pltpu.make_async_copy(pair_hbm.at[parts[i]], pair_ref.at[parts[i]], sems.at[3 + i]))
    for copy in copies:
        copy.start()
    copies[0].wait()
    wide = jnp.concatenate([trial_ref[v].astype(BF16) for v in range(2)], axis=1)
    for device in range(PAIRS):
        out_ref[device, :, : 2 * CB] = wide
    copies[1].wait()
    copies[2].wait()
    for v in range(2):
        gap_ref[HALF * v : HALF * v + HALF] = jnp.broadcast_to(cond_ref[...] - val_ref[v], (HALF, CB))
    projection = jnp.zeros((K, NAUX), F32)
    for i in range(PARTS):
        copies[3 + i].wait()
        rows = slice(2 * CB // PARTS * i, 2 * CB // PARTS * (i + 1))
        projection += dot(wide[:, rows], pair_ref[rows])
    projection = projection.astype(BF16)
    for device in range(PAIRS):
        tile = device // 4
        out_ref[device, :, 2 * CB :] = projection[:, 128 * tile : 128 * tile + 128]


def direct_kernel(first, *refs):
    if first:
        live_ref, arrived_ref, occ_ref, virt_ref, trial_ref, gap_ref = refs[:6]
        out_ref, rows_ref, vectors_ref, blended_ref, total_ref = refs[6:]
    else:
        live_ref, arrived_ref, occ_ref, virt_ref = refs[:4]
        out_ref, vectors_ref, blended_ref, total_ref = refs[4:]
    core, tr, quarter = lax.axis_index("grp"), lax.axis_index("tr"), lax.axis_index("x")

    row = lax.broadcasted_iota(jnp.int32, (HALF * V, 1), 0)
    if first:
        for a in range(AUX):
            for t in range(TR):
                slab = arrived_ref[place(a, t), :, : 2 * CB].astype(F32)
                rows_ref[t, 16 * a : 16 * a + 16] = both_halves(slab).astype(BF16)
        chosen = lax.broadcasted_iota(jnp.int32, (HALF * V, K * V), 1)
        wanted = K * (row % V) + HALF * core + row // V
        wide = rows_ref[tr]
    else:
        chosen = lax.broadcasted_iota(jnp.int32, (HALF * V, HALF * V), 1)
        wanted = HALF * AUX * (row % 2) + HALF * (row % V // 2) + row // V
        slabs = [arrived_ref[place_same_tr(a)].astype(F32) for a in range(AUX)]
        wide = [slabs[a][:, CB * u : CB * u + CB] for u in range(2) for a in range(AUX)]
        wide = jnp.concatenate(wide, axis=0).astype(BF16)
    vectors_ref[...] = dot((chosen == wanted).astype(BF16), wide).astype(BF16)

    live = live_ref[0]
    slot = lax.broadcasted_iota(jnp.int32, (BLOCK * V, V), 0) // V

    def blend(step):
        occ = occ_ref[BLOCK * step : BLOCK * step + BLOCK].reshape(BLOCK * V, V)
        occ = jnp.where(slot < live - step * BLOCK, occ, jnp.zeros_like(occ))
        for k in range(HALF):
            piece = dot(occ, vectors_ref[V * k : V * k + V]).astype(BF16)
            for p in range(BLOCK):
                blended_ref[step % 2, V * k : V * k + V, CB * p : CB * p + CB] = piece[V * p : V * p + V]

    blend(0)
    for step in range(STEPS):
        rows = slice(step * BLOCK * CB, (step + 1) * BLOCK * CB)
        product = dot(blended_ref[step % 2], virt_ref[rows])
        if step + 1 < STEPS:
            blend(step + 1)
        if step == 0:
            total_ref[...] = product
        else:
            total_ref[...] += product

    lanes = lane_ids((K, 128))
    total = total_ref[...].astype(BF16)
    row = lax.broadcasted_iota(jnp.int32, (HALF * AUX, 1), 0)
    chosen = lax.broadcasted_iota(jnp.int32, (HALF * AUX, HALF * V), 1)
    owned = []
    for u in range(2):
        taken = chosen == V * (row % HALF) + 2 * (row // HALF) + u
        owned.append(dot(taken.astype(BF16), total).astype(BF16).astype(F32))
    if first:
        shares = jnp.zeros((K, HALF * V), F32)
        for t in range(TR):
            product = lax.dot_general(
                rows_ref[t], total[:, CB * t : CB * t + CB], NT, preferred_element_type=F32
            ).reshape(V, K, HALF * V)
            mine = lax.broadcasted_iota(jnp.int32, product.shape, 0)
            theirs = lane_ids(product.shape) % V
            shares += jnp.where(mine == theirs, product, 0.0).sum(axis=0)
        group = lane_ids(shares.shape) // V
        kept = jnp.zeros((K, 128), F32)
        for j in range(HALF):
            column = jnp.where(group == j, shares, 0.0).sum(axis=1, keepdims=True)
            for v in range(2):
                vectors = trial_ref[v]
                other = own_rows(core, vectors)[j : j + 1] * gap_ref[HALF * v : HALF * v + 1]
                column += (vectors * other).sum(axis=1, keepdims=True)
            high = column.astype(BF16).astype(F32)
            kept = jnp.where(lanes % 32 == j, high, kept)
            kept = jnp.where(lanes % 32 == HALF + j, column - high, kept)
        projection = jnp.zeros((K, 128), F32)
        for device in range(PAIRS):
            projection += arrived_ref[device, :, 2 * CB :].astype(F32)
        extra = jnp.where(lanes // 32 == quarter, projection, kept)
        near = lax.rem(lanes // 32 - quarter + 4, 4) < 2
        extra = jnp.where(near, extra, pltpu.roll(pltpu.roll(extra, 64, 1), 4, 0))[:HALF]
    else:
        extra = jnp.zeros((HALF, 128), F32)
        for slab in slabs:
            extra += slab[:, 2 * CB :]
    extra = extra.astype(BF16)
    for a in range(AUX):
        for t in range(TR):
            for u in range(2):
                part = owned[u][HALF * a : HALF * a + HALF, CB * t : CB * t + CB]
                out_ref[place(a, t), :, CB * u : CB * u + CB] = part.astype(BF16)
            out_ref[place(a, t), :, 2 * CB :] = extra


def direct_sum(arrived_ref):
    total = jnp.zeros((HALF, 2 * CB), F32)
    for device in range(PAIRS):
        total += arrived_ref[device, :, : 2 * CB].astype(F32)
    return jnp.concatenate([total[:, :CB], total[:, CB:]], axis=0)


def middle_kernel(
    arrived_ref, pair_ref, trial_ref, gap_ref, out_ref, correction_ref, meet_ref
):
    core = lax.axis_index("grp")
    direct = direct_sum(arrived_ref)
    few, lanes = lane_ids((HALF, 128)), lane_ids((K, 128))
    upper = lax.broadcasted_iota(jnp.int32, (K, 128), 0) < HALF
    tiles = []
    sums = [jnp.zeros((HALF, 128), F32) for _ in range(4)]
    for tile in range(TILES):
        low = high = jnp.zeros((HALF, 128), F32)
        for quarter in range(4):
            extra = arrived_ref[4 * tile + quarter, :, 2 * CB :].astype(F32)
            low = jnp.where(few // 32 == quarter, extra, low)
            high = jnp.where(few // 32 == (quarter + 2) % 4, extra, high)
            sums[quarter] += extra
        whole = jnp.concatenate([low, high], axis=0)
        whole = jnp.where(upper, whole, pltpu.roll(whole, 64, 1))
        tiles.append(whole.astype(BF16))
    projection = jnp.concatenate(tiles, axis=1)
    exchange_full = lax.dot_general(projection, pair_ref[...], NT, preferred_element_type=F32)
    mine = own_rows(core, exchange_full)
    exchange = jnp.concatenate([mine[:, :CB], mine[:, CB:]], axis=0)
    low = high = jnp.zeros((HALF, 128), F32)
    for quarter in range(4):
        low = jnp.where(few // 32 == (quarter + 1) % 4, sums[quarter], low)
        high = jnp.where(few // 32 == (quarter + 3) % 4, sums[quarter], high)
    shares = jnp.concatenate([low, high], axis=0)
    meet_exchange = lax.dot_general(projection, projection, NT, preferred_element_type=F32)
    meet = []
    for j in range(HALF):
        column = jnp.where(lanes % 32 % HALF == j, jnp.where(lanes % 32 < K, shares, 0.0), 0.0)
        column = column.sum(axis=1, keepdims=True)
        own = jnp.where(core == 0, meet_exchange[:, j : j + 1], meet_exchange[:, HALF + j : HALF + j + 1])
        meet.append((column + own) / (V * C))
    kept = jnp.zeros((K, 128), F32)
    for j in range(HALF):
        kept = jnp.where(lanes == j, meet[j], kept)
    meet_ref[...] = kept
    gap = gap_ref[...]
    vectors = [trial_ref[v] for v in range(2)]
    trial = jnp.concatenate([own_rows(core, vectors[v]) for v in range(2)], axis=0)
    applied = gap * trial + direct + exchange
    overlap = jnp.concatenate(
        [(vectors[v] * meet[j]).sum(axis=0, keepdims=True) for v in range(2) for j in range(HALF)],
        axis=0,
    )
    correction = (applied - overlap) / gap
    correction_ref[...] = correction
    few = jnp.concatenate([correction[:HALF], correction[HALF:]], axis=1)
    wide = jnp.concatenate([few, jnp.zeros_like(few)], axis=0).astype(BF16)
    projection = dot(wide, pair_ref[...])[:HALF].astype(BF16)
    rounded = few.astype(BF16)
    for a in range(AUX):
        tile = a // 2
        out_ref[a, :, : 2 * CB] = rounded
        out_ref[a, :, 2 * CB :] = projection[:, 128 * tile : 128 * tile + 128]


def last_kernel(arrived_ref, pair_ref, correction_ref, gap_ref, meet_ref, out_ref):
    direct = direct_sum(arrived_ref)
    tiles = []
    for tile in range(TILES):
        at = tile // 8 * 32 + 2 * tile % 16
        tiles.append(arrived_ref[at, :, 2 * CB :].astype(F32) + arrived_ref[at + 16, :, 2 * CB :].astype(F32))
    few = jnp.concatenate(tiles, axis=1)
    projection = jnp.concatenate([few, jnp.zeros_like(few)], axis=0).astype(BF16)
    exchange = lax.dot_general(projection, pair_ref[...], NT, preferred_element_type=F32)
    exchange = jnp.concatenate([exchange[:HALF, :CB], exchange[:HALF, CB:]], axis=0)
    out_ref[:, :CB] = gap_ref[...] * correction_ref[...] + direct + exchange
    out_ref[:, CB:] = meet_ref[...]


def join_kernel(both_ref, applied_ref, meet_ref):
    for v in range(2):
        rows = [both_ref[core, HALF * v : HALF * v + HALF, :CB] for core in range(2)]
        applied_ref[v] = jnp.concatenate(rows, axis=0)
    columns = [both_ref[core, :, CB : CB + HALF] for core in range(2)]
    meet_ref[...] = jnp.concatenate(columns, axis=1)


def direct_call(first, live, arrived, occ, virt, *local):
    out = jax.ShapeDtypeStruct((PAIRS, HALF, 2 * CB + 128), BF16)
    scratch = [
        pltpu.VMEM((HALF * V, CB), BF16),
        pltpu.VMEM((2, HALF * V, BLOCK * CB), BF16),
        pltpu.VMEM((HALF * V, C), F32),
    ]
    if first:
        scratch = [pltpu.VMEM((TR, K * V, CB), BF16), *scratch]
    return pl.pallas_call(
        functools.partial(direct_kernel, first),
        in_specs=[SMEM] + [VMEM] * (5 if first else 3),
        out_specs=VMEM,
        out_shape=out,
        scratch_shapes=scratch,
        compiler_params=params(12),
    )(live, arrived, occ, virt, *local)


def body(trial_vectors, energy_val, energy_cond, coef_occ, coef_virt, pair_coef, live_aux):
    pair = pair_coef.reshape(2 * CB, NAUX)
    virt = coef_virt.reshape(SLOTS * CB, C)
    cond = energy_cond.reshape(1, CB)

    def exchange(x, axes):
        return lax.all_to_all(x, axes, split_axis=0, concat_axis=0, tiled=True)

    sent, trial, gap, pair = pl.pallas_call(
        first_kernel,
        in_specs=[SMEM] + [HBM] * 4,
        out_specs=[VMEM] * 4,
        out_shape=[
            jax.ShapeDtypeStruct((PAIRS, K, 2 * CB + 128), BF16),
            jax.ShapeDtypeStruct((2, K, CB), F32),
            jax.ShapeDtypeStruct((2 * HALF, CB), F32),
            jax.typeof(pair),
        ],
        scratch_shapes=[
            pltpu.VMEM((1, CB), F32),
            pltpu.SMEM((2,), F32),
            pltpu.SemaphoreType.DMA((3 + PARTS,)),
        ],
        cost_estimate=pl.CostEstimate(flops=UNTIL_DIRECT, bytes_accessed=2 * pair.size, transcendentals=0),
        compiler_params=params(8),
    )(live_aux, *(stays(x) for x in (trial_vectors, pair, cond, energy_val)))
    arrived = exchange(sent, ALL)
    sent = direct_call(True, live_aux, arrived, coef_occ, virt, trial, gap)
    arrived = exchange(sent, ALL)
    sent, correction, meet = pl.pallas_call(
        middle_kernel,
        in_specs=[VMEM] * 4,
        out_specs=[VMEM] * 3,
        out_shape=[
            jax.ShapeDtypeStruct((AUX, HALF, 2 * CB + 128), BF16),
            jax.ShapeDtypeStruct((2 * HALF, CB), F32),
            jax.ShapeDtypeStruct((K, 128), F32),
        ],
        compiler_params=params(8),
    )(arrived, pair, trial, gap)
    arrived = exchange(sent, SAME_TR)
    sent = direct_call(False, live_aux, arrived, coef_occ, virt)
    arrived = exchange(sent, ALL)
    mine = pl.pallas_call(
        last_kernel,
        in_specs=[VMEM] * 5,
        out_specs=VMEM,
        out_shape=jax.ShapeDtypeStruct((2 * HALF, CB + 128), F32),
        compiler_params=params(8),
    )(arrived, pair, correction, gap, meet)
    both = lax.all_gather(mine, "grp")
    applied, intersection = pl.pallas_call(
        join_kernel,
        in_specs=[VMEM],
        out_specs=[VMEM] * 2,
        out_shape=[jax.ShapeDtypeStruct((2, K, CB), F32), jax.ShapeDtypeStruct((K, K), F32)],
        compiler_params=params(4),
    )(both)
    return (applied, intersection)


def solution(mesh):
    mesh = Mesh(mesh.devices.reshape(2, 4, 2, 4, TR), ("grp", "y", "zh", "x", "tr"))
    aux = ("y", "zh", "x")
    in_specs = (
        P(aux, None, "tr"),
        P(aux),
        P("tr"),
        P(aux, None, None),
        P(aux, "tr", None),
        P(aux, "tr", None),
        P(aux),
    )
    out_specs = (P(aux, None, "tr"), P())
    return jax.shard_map(body, mesh=mesh, in_specs=in_specs, out_specs=out_specs, check_vma=False)
```

```python
import functools

import jax
import jax.numpy as jnp
from jax import lax
from jax.experimental import pallas as pl
from jax.experimental.pallas import tpu as pltpu
from jax.sharding import Mesh
from jax.sharding import PartitionSpec as P

V = 64
C = 512
K = 8
HALF = 4
AUX = 32
TR = 2
CB = C // TR
PAIRS = AUX * TR
ALL = ("zh", "tr", "y", "x")
SAME_TR = ("zh", "y", "x")
SLOTS = 64
NAUX = 2048
BLOCK = 16
STEPS = SLOTS // BLOCK
PARTS = 4
UNTIL_DIRECT = 2 * 10**10
TILES = NAUX // 128
F32 = jnp.float32
BF16 = jnp.bfloat16
VMEM = pl.BlockSpec(memory_space=pltpu.VMEM)
SMEM = pl.BlockSpec(memory_space=pltpu.SMEM)
HBM = pl.BlockSpec(memory_space=pltpu.HBM)
NT = (((1,), (1,)), ((), ()))


def place(a, t):
    y, zh, x = a // 8, a // 4 % 2, a % 4
    return zh * 32 + t * 16 + y * 4 + x


def place_same_tr(a):
    y, zh, x = a // 8, a // 4 % 2, a % 4
    return zh * 16 + y * 4 + x


def stays(x):
    return pltpu.with_memory_space_constraint(x, pltpu.HBM)


def params(mib):
    return pltpu.CompilerParams(vmem_limit_bytes=mib * 2**20)


def dot(a, b):
    return jnp.dot(a, b, preferred_element_type=F32)


def lane_ids(shape):
    return lax.broadcasted_iota(jnp.int32, shape, len(shape) - 1)


def own_rows(core, rows):
    return jnp.where(core == 0, rows[:HALF], rows[HALF:])


def both_halves(rows):
    return jnp.concatenate([rows[:, :CB], rows[:, CB : 2 * CB]], axis=0)


def first_kernel(
    live_ref, trial_hbm, pair_hbm, cond_hbm, val_hbm, out_ref, trial_ref, gap_ref, pair_ref, cond_ref, val_ref, sems
):
    parts = [pl.ds(2 * CB // PARTS * i, 2 * CB // PARTS) for i in range(PARTS)]
    copies = [
        pltpu.make_async_copy(trial_hbm, trial_ref, sems.at[0]),
        pltpu.make_async_copy(cond_hbm, cond_ref, sems.at[1]),
        pltpu.make_async_copy(val_hbm, val_ref, sems.at[2]),
    ]
    for i in range(PARTS):
        copies.append(pltpu.make_async_copy(pair_hbm.at[parts[i]], pair_ref.at[parts[i]], sems.at[3 + i]))
    for copy in copies:
        copy.start()
    copies[0].wait()
    wide = jnp.concatenate([trial_ref[v].astype(BF16) for v in range(2)], axis=1)
    for device in range(PAIRS):
        out_ref[device, :, : 2 * CB] = wide
    copies[1].wait()
    copies[2].wait()
    for v in range(2):
        gap_ref[HALF * v : HALF * v + HALF] = jnp.broadcast_to(cond_ref[...] - val_ref[v], (HALF, CB))
    projection = jnp.zeros((K, NAUX), F32)
    for i in range(PARTS):
        copies[3 + i].wait()
        rows = slice(2 * CB // PARTS * i, 2 * CB // PARTS * (i + 1))
        projection += dot(wide[:, rows], pair_ref[rows])
    projection = projection.astype(BF16)
    for device in range(PAIRS):
        tile = device // 4
        out_ref[device, :, 2 * CB :] = projection[:, 128 * tile : 128 * tile + 128]


def direct_kernel(first, *refs):
    if first:
        live_ref, arrived_ref, occ_ref, virt_ref, trial_ref, gap_ref = refs[:6]
        out_ref, rows_ref, vectors_ref, blended_ref, total_ref = refs[6:]
    else:
        live_ref, arrived_ref, occ_ref, virt_ref = refs[:4]
        out_ref, vectors_ref, blended_ref, total_ref = refs[4:]
    core, tr, quarter = lax.axis_index("grp"), lax.axis_index("tr"), lax.axis_index("x")

    row = lax.broadcasted_iota(jnp.int32, (HALF * V, 1), 0)
    if first:
        chosen = lax.broadcasted_iota(jnp.int32, (HALF * V, K * V), 1)
        wanted = K * (row % V) + HALF * core + row // V
        stride = place(0, 1) - place(0, 0)
        wide = [arrived_ref[place(a, 0) + stride * tr, :, : 2 * CB].astype(F32) for a in range(AUX)]
        wide = jnp.concatenate([both_halves(slab) for slab in wide], axis=0).astype(BF16)
        projection = jnp.zeros((K, 128), F32)
    else:
        chosen = lax.broadcasted_iota(jnp.int32, (HALF * V, HALF * V), 1)
        wanted = HALF * AUX * (row % 2) + HALF * (row % V // 2) + row // V
        slabs = [arrived_ref[place_same_tr(a)].astype(F32) for a in range(AUX)]
        wide = [slabs[a][:, CB * u : CB * u + CB] for u in range(2) for a in range(AUX)]
        wide = jnp.concatenate(wide, axis=0).astype(BF16)
    vectors_ref[...] = dot((chosen == wanted).astype(BF16), wide).astype(BF16)

    live = live_ref[0]
    slot = lax.broadcasted_iota(jnp.int32, (BLOCK * V, V), 0) // V

    def blend(step):
        occ = occ_ref[BLOCK * step : BLOCK * step + BLOCK].reshape(BLOCK * V, V)
        occ = jnp.where(slot < live - step * BLOCK, occ, jnp.zeros_like(occ))
        for k in range(HALF):
            piece = dot(occ, vectors_ref[V * k : V * k + V]).astype(BF16)
            for p in range(BLOCK):
                blended_ref[step % 2, V * k : V * k + V, CB * p : CB * p + CB] = piece[V * p : V * p + V]

    blend(0)
    devices = [(a, t) for a in range(AUX) for t in range(TR)]
    for step in range(STEPS):
        rows = slice(step * BLOCK * CB, (step + 1) * BLOCK * CB)
        product = dot(blended_ref[step % 2], virt_ref[rows])
        if step + 1 < STEPS:
            blend(step + 1)
        if first:
            for a, t in devices[step::STEPS]:
                slab = arrived_ref[place(a, t)].astype(F32)
                rows_ref[t, 16 * a : 16 * a + 16] = both_halves(slab).astype(BF16)
                projection += slab[:, 2 * CB :]
        if step == 0:
            total_ref[...] = product
        else:
            total_ref[...] += product

    lanes = lane_ids((K, 128))
    total = total_ref[...].astype(BF16)
    row = lax.broadcasted_iota(jnp.int32, (HALF * AUX, 1), 0)
    chosen = lax.broadcasted_iota(jnp.int32, (HALF * AUX, HALF * V), 1)
    owned = []
    for u in range(2):
        taken = chosen == V * (row % HALF) + 2 * (row // HALF) + u
        owned.append(dot(taken.astype(BF16), total).astype(BF16).astype(F32))
    if first:
        shares = jnp.zeros((K, HALF * V), F32)
        for t in range(TR):
            product = lax.dot_general(
                rows_ref[t], total[:, CB * t : CB * t + CB], NT, preferred_element_type=F32
            ).reshape(V, K, HALF * V)
            mine = lax.broadcasted_iota(jnp.int32, product.shape, 0)
            theirs = lane_ids(product.shape) % V
            shares += jnp.where(mine == theirs, product, 0.0).sum(axis=0)
        group = lane_ids(shares.shape) // V
        kept = jnp.zeros((K, 128), F32)
        for j in range(HALF):
            column = jnp.where(group == j, shares, 0.0).sum(axis=1, keepdims=True)
            for v in range(2):
                vectors = trial_ref[v]
                other = own_rows(core, vectors)[j : j + 1] * gap_ref[HALF * v : HALF * v + 1]
                column += (vectors * other).sum(axis=1, keepdims=True)
            high = column.astype(BF16).astype(F32)
            kept = jnp.where(lanes % 32 == j, high, kept)
            kept = jnp.where(lanes % 32 == HALF + j, column - high, kept)
        extra = jnp.where(lanes // 32 == quarter, projection, kept)
        near = lax.rem(lanes // 32 - quarter + 4, 4) < 2
        extra = jnp.where(near, extra, pltpu.roll(pltpu.roll(extra, 64, 1), 4, 0))[:HALF]
    else:
        extra = jnp.zeros((HALF, 128), F32)
        for slab in slabs:
            extra += slab[:, 2 * CB :]
    extra = extra.astype(BF16)
    for a in range(AUX):
        for t in range(TR):
            for u in range(2):
                part = owned[u][HALF * a : HALF * a + HALF, CB * t : CB * t + CB]
                out_ref[place(a, t), :, CB * u : CB * u + CB] = part.astype(BF16)
            out_ref[place(a, t), :, 2 * CB :] = extra


def direct_sum(arrived_ref):
    total = jnp.zeros((HALF, 2 * CB), F32)
    for device in range(PAIRS):
        total += arrived_ref[device, :, : 2 * CB].astype(F32)
    return jnp.concatenate([total[:, :CB], total[:, CB:]], axis=0)


def middle_kernel(
    arrived_ref, pair_ref, trial_ref, gap_ref, out_ref, correction_ref, meet_ref
):
    core = lax.axis_index("grp")
    direct = direct_sum(arrived_ref)
    few, lanes = lane_ids((HALF, 128)), lane_ids((K, 128))
    upper = lax.broadcasted_iota(jnp.int32, (K, 128), 0) < HALF
    tiles = []
    sums = [jnp.zeros((HALF, 128), F32) for _ in range(4)]
    for tile in range(TILES):
        low = high = jnp.zeros((HALF, 128), F32)
        for quarter in range(4):
            extra = arrived_ref[4 * tile + quarter, :, 2 * CB :].astype(F32)
            low = jnp.where(few // 32 == quarter, extra, low)
            high = jnp.where(few // 32 == (quarter + 2) % 4, extra, high)
            sums[quarter] += extra
        whole = jnp.concatenate([low, high], axis=0)
        whole = jnp.where(upper, whole, pltpu.roll(whole, 64, 1))
        tiles.append(whole.astype(BF16))
    projection = jnp.concatenate(tiles, axis=1)
    exchange_full = lax.dot_general(projection, pair_ref[...], NT, preferred_element_type=F32)
    mine = own_rows(core, exchange_full)
    exchange = jnp.concatenate([mine[:, :CB], mine[:, CB:]], axis=0)
    low = high = jnp.zeros((HALF, 128), F32)
    for quarter in range(4):
        low = jnp.where(few // 32 == (quarter + 1) % 4, sums[quarter], low)
        high = jnp.where(few // 32 == (quarter + 3) % 4, sums[quarter], high)
    shares = jnp.concatenate([low, high], axis=0)
    meet_exchange = lax.dot_general(projection, projection, NT, preferred_element_type=F32)
    meet = []
    for j in range(HALF):
        column = jnp.where(lanes % 32 % HALF == j, jnp.where(lanes % 32 < K, shares, 0.0), 0.0)
        column = column.sum(axis=1, keepdims=True)
        own = jnp.where(core == 0, meet_exchange[:, j : j + 1], meet_exchange[:, HALF + j : HALF + j + 1])
        meet.append((column + own) / (V * C))
    kept = jnp.zeros((K, 128), F32)
    for j in range(HALF):
        kept = jnp.where(lanes == j, meet[j], kept)
    meet_ref[...] = kept
    gap = gap_ref[...]
    vectors = [trial_ref[v] for v in range(2)]
    trial = jnp.concatenate([own_rows(core, vectors[v]) for v in range(2)], axis=0)
    applied = gap * trial + direct + exchange
    overlap = jnp.concatenate(
        [(vectors[v] * meet[j]).sum(axis=0, keepdims=True) for v in range(2) for j in range(HALF)],
        axis=0,
    )
    correction = (applied - overlap) / gap
    correction_ref[...] = correction
    few = jnp.concatenate([correction[:HALF], correction[HALF:]], axis=1)
    wide = jnp.concatenate([few, jnp.zeros_like(few)], axis=0).astype(BF16)
    projection = dot(wide, pair_ref[...])[:HALF].astype(BF16)
    rounded = few.astype(BF16)
    for a in range(AUX):
        tile = a // 2
        out_ref[a, :, : 2 * CB] = rounded
        out_ref[a, :, 2 * CB :] = projection[:, 128 * tile : 128 * tile + 128]


def last_kernel(arrived_ref, pair_ref, correction_ref, gap_ref, meet_ref, out_ref):
    direct = direct_sum(arrived_ref)
    tiles = []
    for tile in range(TILES):
        at = tile // 8 * 32 + 2 * tile % 16
        tiles.append(arrived_ref[at, :, 2 * CB :].astype(F32) + arrived_ref[at + 16, :, 2 * CB :].astype(F32))
    few = jnp.concatenate(tiles, axis=1)
    projection = jnp.concatenate([few, jnp.zeros_like(few)], axis=0).astype(BF16)
    exchange = lax.dot_general(projection, pair_ref[...], NT, preferred_element_type=F32)
    exchange = jnp.concatenate([exchange[:HALF, :CB], exchange[:HALF, CB:]], axis=0)
    out_ref[:, :CB] = gap_ref[...] * correction_ref[...] + direct + exchange
    out_ref[:, CB:] = meet_ref[...]


def join_kernel(both_ref, applied_ref, meet_ref):
    for v in range(2):
        rows = [both_ref[core, HALF * v : HALF * v + HALF, :CB] for core in range(2)]
        applied_ref[v] = jnp.concatenate(rows, axis=0)
    columns = [both_ref[core, :, CB : CB + HALF] for core in range(2)]
    meet_ref[...] = jnp.concatenate(columns, axis=1)


def direct_call(first, live, arrived, occ, virt, *local):
    out = jax.ShapeDtypeStruct((PAIRS, HALF, 2 * CB + 128), BF16)
    scratch = [
        pltpu.VMEM((HALF * V, CB), BF16),
        pltpu.VMEM((2, HALF * V, BLOCK * CB), BF16),
        pltpu.VMEM((HALF * V, C), F32),
    ]
    if first:
        scratch = [pltpu.VMEM((TR, K * V, CB), BF16), *scratch]
    return pl.pallas_call(
        functools.partial(direct_kernel, first),
        in_specs=[SMEM] + [VMEM] * (5 if first else 3),
        out_specs=VMEM,
        out_shape=out,
        scratch_shapes=scratch,
        compiler_params=params(20),
    )(live, arrived, occ, virt, *local)


def body(trial_vectors, energy_val, energy_cond, coef_occ, coef_virt, pair_coef, live_aux):
    pair = pair_coef.reshape(2 * CB, NAUX)
    virt = coef_virt.reshape(SLOTS * CB, C)
    cond = energy_cond.reshape(1, CB)

    def exchange(x, axes):
        return lax.all_to_all(x, axes, split_axis=0, concat_axis=0, tiled=True)

    sent, trial, gap, pair = pl.pallas_call(
        first_kernel,
        in_specs=[SMEM] + [HBM] * 4,
        out_specs=[VMEM] * 4,
        out_shape=[
            jax.ShapeDtypeStruct((PAIRS, K, 2 * CB + 128), BF16),
            jax.ShapeDtypeStruct((2, K, CB), F32),
            jax.ShapeDtypeStruct((2 * HALF, CB), F32),
            jax.typeof(pair),
        ],
        scratch_shapes=[
            pltpu.VMEM((1, CB), F32),
            pltpu.SMEM((2,), F32),
            pltpu.SemaphoreType.DMA((3 + PARTS,)),
        ],
        cost_estimate=pl.CostEstimate(flops=UNTIL_DIRECT, bytes_accessed=2 * pair.size, transcendentals=0),
        compiler_params=params(8),
    )(live_aux, *(stays(x) for x in (trial_vectors, pair, cond, energy_val)))
    arrived = exchange(sent, ALL)
    sent = direct_call(True, live_aux, arrived, coef_occ, virt, trial, gap)
    arrived = exchange(sent, ALL)
    sent, correction, meet = pl.pallas_call(
        middle_kernel,
        in_specs=[VMEM] * 4,
        out_specs=[VMEM] * 3,
        out_shape=[
            jax.ShapeDtypeStruct((AUX, HALF, 2 * CB + 128), BF16),
            jax.ShapeDtypeStruct((2 * HALF, CB), F32),
            jax.ShapeDtypeStruct((K, 128), F32),
        ],
        compiler_params=params(8),
    )(arrived, pair, trial, gap)
    arrived = exchange(sent, SAME_TR)
    sent = direct_call(False, live_aux, arrived, coef_occ, virt)
    arrived = exchange(sent, ALL)
    mine = pl.pallas_call(
        last_kernel,
        in_specs=[VMEM] * 5,
        out_specs=VMEM,
        out_shape=jax.ShapeDtypeStruct((2 * HALF, CB + 128), F32),
        compiler_params=params(8),
    )(arrived, pair, correction, gap, meet)
    both = lax.all_gather(mine, "grp")
    applied, intersection = pl.pallas_call(
        join_kernel,
        in_specs=[VMEM],
        out_specs=[VMEM] * 2,
        out_shape=[jax.ShapeDtypeStruct((2, K, CB), F32), jax.ShapeDtypeStruct((K, K), F32)],
        compiler_params=params(4),
    )(both)
    return (applied, intersection)


def solution(mesh):
    mesh = Mesh(mesh.devices.reshape(2, 4, 2, 4, TR), ("grp", "y", "zh", "x", "tr"))
    aux = ("y", "zh", "x")
    in_specs = (
        P(aux, None, "tr"),
        P(aux),
        P("tr"),
        P(aux, None, None),
        P(aux, "tr", None),
        P(aux, "tr", None),
        P(aux),
    )
    out_specs = (P(aux, None, "tr"), P())
    return jax.shard_map(body, mesh=mesh, in_specs=in_specs, out_specs=out_specs, check_vma=False)
```

```python
import functools

import jax
import jax.numpy as jnp
from jax import lax
from jax.experimental import pallas as pl
from jax.experimental.pallas import tpu as pltpu
from jax.sharding import Mesh
from jax.sharding import PartitionSpec as P

V = 64
C = 512
K = 8
HALF = 4
AUX = 32
TR = 2
CB = C // TR
PAIRS = AUX * TR
ALL = ("zh", "tr", "y", "x")
SAME_TR = ("zh", "y", "x")
SLOTS = 64
NAUX = 2048
BLOCK = 16
STEPS = SLOTS // BLOCK
PARTS = 4
UNTIL_DIRECT = 2 * 10**10
TILES = NAUX // 128
F32 = jnp.float32
BF16 = jnp.bfloat16
VMEM = pl.BlockSpec(memory_space=pltpu.VMEM)
SMEM = pl.BlockSpec(memory_space=pltpu.SMEM)
HBM = pl.BlockSpec(memory_space=pltpu.HBM)
NT = (((1,), (1,)), ((), ()))


def place(a, t):
    y, zh, x = a // 8, a // 4 % 2, a % 4
    return zh * 32 + t * 16 + y * 4 + x


def place_same_tr(a):
    y, zh, x = a // 8, a // 4 % 2, a % 4
    return zh * 16 + y * 4 + x


def stays(x):
    return pltpu.with_memory_space_constraint(x, pltpu.HBM)


def params(mib):
    return pltpu.CompilerParams(vmem_limit_bytes=mib * 2**20)


def dot(a, b):
    return jnp.dot(a, b, preferred_element_type=F32)


def lane_ids(shape):
    return lax.broadcasted_iota(jnp.int32, shape, len(shape) - 1)


def own_rows(core, rows):
    return jnp.where(core == 0, rows[:HALF], rows[HALF:])


def both_halves(slab):
    parts = [slab[:, CB * i : CB * i + CB] for i in (0, 2, 1, 3)]
    return jnp.concatenate(parts, axis=0)


def first_kernel(
    live_ref, trial_hbm, pair_hbm, cond_hbm, val_hbm, out_ref, trial_ref, gap_ref, pair_ref, cond_ref, val_ref, sems
):
    parts = [pl.ds(2 * CB // PARTS * i, 2 * CB // PARTS) for i in range(PARTS)]
    copies = [
        pltpu.make_async_copy(trial_hbm, trial_ref, sems.at[0]),
        pltpu.make_async_copy(cond_hbm, cond_ref, sems.at[1]),
        pltpu.make_async_copy(val_hbm, val_ref, sems.at[2]),
    ]
    for i in range(PARTS):
        copies.append(pltpu.make_async_copy(pair_hbm.at[parts[i]], pair_ref.at[parts[i]], sems.at[3 + i]))
    for copy in copies:
        copy.start()
    copies[0].wait()
    wide = jnp.concatenate([trial_ref[v].astype(BF16) for v in range(2)], axis=1)
    few = wide.astype(F32)
    few = jnp.concatenate([few[:HALF], few[HALF:]], axis=1).astype(BF16)
    for device in range(PAIRS):
        out_ref[device, :, : 4 * CB] = few
    copies[1].wait()
    copies[2].wait()
    for v in range(2):
        gap_ref[HALF * v : HALF * v + HALF] = jnp.broadcast_to(cond_ref[...] - val_ref[v], (HALF, CB))
    projection = jnp.zeros((K, NAUX), F32)
    for i in range(PARTS):
        copies[3 + i].wait()
        rows = slice(2 * CB // PARTS * i, 2 * CB // PARTS * (i + 1))
        projection += dot(wide[:, rows], pair_ref[rows])
    lanes = lane_ids((HALF, 128))
    for tile in range(TILES):
        part = projection[:, 128 * tile : 128 * tile + 128]
        low, high = part[:HALF], pltpu.roll(part, 64, 1)[HALF:]
        for quarter in range(4):
            both = jnp.where(lanes // 32 == quarter, low, high)
            out_ref[4 * tile + quarter, :, 4 * CB :] = both.astype(BF16)


def direct_kernel(first, *refs):
    if first:
        live_ref, arrived_ref, occ_ref, virt_ref, trial_ref, gap_ref = refs[:6]
        out_ref, rows_ref, vectors_ref, blended_ref, total_ref = refs[6:]
    else:
        live_ref, arrived_ref, occ_ref, virt_ref = refs[:4]
        out_ref, vectors_ref, blended_ref, total_ref = refs[4:]
    core, tr, quarter = lax.axis_index("grp"), lax.axis_index("tr"), lax.axis_index("x")

    row = lax.broadcasted_iota(jnp.int32, (HALF * V, 1), 0)
    if first:
        chosen = lax.broadcasted_iota(jnp.int32, (HALF * V, K * V), 1)
        wanted = K * (row % V) + HALF * core + row // V
        stride = place(0, 1) - place(0, 0)
        wide = [arrived_ref[place(a, 0) + stride * tr].astype(F32) for a in range(AUX)]
        wide = jnp.concatenate([both_halves(slab) for slab in wide], axis=0).astype(BF16)
        projection = jnp.zeros((HALF, 128), F32)
    else:
        chosen = lax.broadcasted_iota(jnp.int32, (HALF * V, HALF * V), 1)
        wanted = HALF * AUX * (row % 2) + HALF * (row % V // 2) + row // V
        slabs = [arrived_ref[place_same_tr(a)].astype(F32) for a in range(AUX)]
        wide = [slabs[a][:, CB * u : CB * u + CB] for u in range(2) for a in range(AUX)]
        wide = jnp.concatenate(wide, axis=0).astype(BF16)
    vectors_ref[...] = dot((chosen == wanted).astype(BF16), wide).astype(BF16)

    live = live_ref[0]
    slot = lax.broadcasted_iota(jnp.int32, (BLOCK * V, V), 0) // V

    def blend(step):
        occ = occ_ref[BLOCK * step : BLOCK * step + BLOCK].reshape(BLOCK * V, V)
        occ = jnp.where(slot < live - step * BLOCK, occ, jnp.zeros_like(occ))
        for k in range(HALF):
            piece = dot(occ, vectors_ref[V * k : V * k + V]).astype(BF16)
            for p in range(BLOCK):
                blended_ref[step % 2, V * k : V * k + V, CB * p : CB * p + CB] = piece[V * p : V * p + V]

    blend(0)
    devices = [(a, t) for a in range(AUX) for t in range(TR)]
    for step in range(STEPS):
        rows = slice(step * BLOCK * CB, (step + 1) * BLOCK * CB)
        product = dot(blended_ref[step % 2], virt_ref[rows])
        if step + 1 < STEPS:
            blend(step + 1)
        if first:
            for a, t in devices[step::STEPS]:
                slab = arrived_ref[place(a, t)].astype(F32)
                rows_ref[t, 16 * a : 16 * a + 16] = both_halves(slab).astype(BF16)
                projection += slab[:, 4 * CB :]
        if step == 0:
            total_ref[...] = product
        else:
            total_ref[...] += product

    lanes = lane_ids((K, 128))
    total = total_ref[...].astype(BF16)
    row = lax.broadcasted_iota(jnp.int32, (HALF * AUX, 1), 0)
    chosen = lax.broadcasted_iota(jnp.int32, (HALF * AUX, HALF * V), 1)
    owned = []
    for u in range(2):
        taken = chosen == V * (row % HALF) + 2 * (row // HALF) + u
        owned.append(dot(taken.astype(BF16), total).astype(BF16).astype(F32))
    if first:
        shares = jnp.zeros((K, HALF * V), F32)
        for t in range(TR):
            product = lax.dot_general(
                rows_ref[t], total[:, CB * t : CB * t + CB], NT, preferred_element_type=F32
            ).reshape(V, K, HALF * V)
            mine = lax.broadcasted_iota(jnp.int32, product.shape, 0)
            theirs = lane_ids(product.shape) % V
            shares += jnp.where(mine == theirs, product, 0.0).sum(axis=0)
        group = lane_ids(shares.shape) // V
        kept = jnp.zeros((K, 128), F32)
        for j in range(HALF):
            column = jnp.where(group == j, shares, 0.0).sum(axis=1, keepdims=True)
            for v in range(2):
                vectors = trial_ref[v]
                other = own_rows(core, vectors)[j : j + 1] * gap_ref[HALF * v : HALF * v + 1]
                column += (vectors * other).sum(axis=1, keepdims=True)
            high = column.astype(BF16).astype(F32)
            kept = jnp.where(lanes % 32 == j, high, kept)
            kept = jnp.where(lanes % 32 == HALF + j, column - high, kept)
        ahead = lax.rem(lanes // 32 - quarter + 4, 4)
        kept = jnp.where(ahead < 2, kept, pltpu.roll(kept, 4, 0))[:HALF]
        extra = jnp.where(ahead[:HALF] % 2 == 0, projection, kept)
    else:
        extra = jnp.zeros((HALF, 128), F32)
        for slab in slabs:
            extra += slab[:, 2 * CB :]
    extra = extra.astype(BF16)
    for a in range(AUX):
        for t in range(TR):
            for u in range(2):
                part = owned[u][HALF * a : HALF * a + HALF, CB * t : CB * t + CB]
                out_ref[place(a, t), :, CB * u : CB * u + CB] = part.astype(BF16)
            out_ref[place(a, t), :, 2 * CB :] = extra


def direct_sum(arrived_ref):
    total = jnp.zeros((HALF, 2 * CB), F32)
    for device in range(PAIRS):
        total += arrived_ref[device, :, : 2 * CB].astype(F32)
    return jnp.concatenate([total[:, :CB], total[:, CB:]], axis=0)


def middle_kernel(
    arrived_ref, pair_ref, trial_ref, gap_ref, out_ref, correction_ref, meet_ref
):
    core = lax.axis_index("grp")
    direct = direct_sum(arrived_ref)
    few, lanes = lane_ids((HALF, 128)), lane_ids((K, 128))
    upper = lax.broadcasted_iota(jnp.int32, (K, 128), 0) < HALF
    tiles = []
    sums = [jnp.zeros((HALF, 128), F32) for _ in range(4)]
    for tile in range(TILES):
        low = high = jnp.zeros((HALF, 128), F32)
        for quarter in range(4):
            extra = arrived_ref[4 * tile + quarter, :, 2 * CB :].astype(F32)
            low = jnp.where(few // 32 == quarter, extra, low)
            high = jnp.where(few // 32 == (quarter + 2) % 4, extra, high)
            sums[quarter] += extra
        whole = jnp.concatenate([low, high], axis=0)
        whole = jnp.where(upper, whole, pltpu.roll(whole, 64, 1))
        tiles.append(whole.astype(BF16))
    projection = jnp.concatenate(tiles, axis=1)
    exchange_full = lax.dot_general(projection, pair_ref[...], NT, preferred_element_type=F32)
    mine = own_rows(core, exchange_full)
    exchange = jnp.concatenate([mine[:, :CB], mine[:, CB:]], axis=0)
    low = high = jnp.zeros((HALF, 128), F32)
    for quarter in range(4):
        low = jnp.where(few // 32 == (quarter + 1) % 4, sums[quarter], low)
        high = jnp.where(few // 32 == (quarter + 3) % 4, sums[quarter], high)
    shares = jnp.concatenate([low, high], axis=0)
    meet_exchange = lax.dot_general(projection, projection, NT, preferred_element_type=F32)
    meet = []
    for j in range(HALF):
        column = jnp.where(lanes % 32 % HALF == j, jnp.where(lanes % 32 < K, shares, 0.0), 0.0)
        column = column.sum(axis=1, keepdims=True)
        own = jnp.where(core == 0, meet_exchange[:, j : j + 1], meet_exchange[:, HALF + j : HALF + j + 1])
        meet.append((column + own) / (V * C))
    kept = jnp.zeros((K, 128), F32)
    for j in range(HALF):
        kept = jnp.where(lanes == j, meet[j], kept)
    meet_ref[...] = kept
    gap = gap_ref[...]
    vectors = [trial_ref[v] for v in range(2)]
    trial = jnp.concatenate([own_rows(core, vectors[v]) for v in range(2)], axis=0)
    applied = gap * trial + direct + exchange
    overlap = jnp.concatenate(
        [(vectors[v] * meet[j]).sum(axis=0, keepdims=True) for v in range(2) for j in range(HALF)],
        axis=0,
    )
    correction = (applied - overlap) / gap
    correction_ref[...] = correction
    few = jnp.concatenate([correction[:HALF], correction[HALF:]], axis=1)
    wide = jnp.concatenate([few, jnp.zeros_like(few)], axis=0).astype(BF16)
    projection = dot(wide, pair_ref[...])[:HALF].astype(BF16)
    rounded = few.astype(BF16)
    for a in range(AUX):
        tile = a // 2
        out_ref[a, :, : 2 * CB] = rounded
        out_ref[a, :, 2 * CB :] = projection[:, 128 * tile : 128 * tile + 128]


def last_kernel(arrived_ref, pair_ref, correction_ref, gap_ref, meet_ref, out_ref):
    direct = direct_sum(arrived_ref)
    tiles = []
    for tile in range(TILES):
        at = tile // 8 * 32 + 2 * tile % 16
        tiles.append(arrived_ref[at, :, 2 * CB :].astype(F32) + arrived_ref[at + 16, :, 2 * CB :].astype(F32))
    few = jnp.concatenate(tiles, axis=1)
    projection = jnp.concatenate([few, jnp.zeros_like(few)], axis=0).astype(BF16)
    exchange = lax.dot_general(projection, pair_ref[...], NT, preferred_element_type=F32)
    exchange = jnp.concatenate([exchange[:HALF, :CB], exchange[:HALF, CB:]], axis=0)
    out_ref[:, :CB] = gap_ref[...] * correction_ref[...] + direct + exchange
    out_ref[:, CB:] = meet_ref[...]


def join_kernel(both_ref, applied_ref, meet_ref):
    for v in range(2):
        rows = [both_ref[core, HALF * v : HALF * v + HALF, :CB] for core in range(2)]
        applied_ref[v] = jnp.concatenate(rows, axis=0)
    columns = [both_ref[core, :, CB : CB + HALF] for core in range(2)]
    meet_ref[...] = jnp.concatenate(columns, axis=1)


def direct_call(first, live, arrived, occ, virt, *local):
    out = jax.ShapeDtypeStruct((PAIRS, HALF, 2 * CB + 128), BF16)
    scratch = [
        pltpu.VMEM((HALF * V, CB), BF16),
        pltpu.VMEM((2, HALF * V, BLOCK * CB), BF16),
        pltpu.VMEM((HALF * V, C), F32),
    ]
    if first:
        scratch = [pltpu.VMEM((TR, K * V, CB), BF16), *scratch]
    return pl.pallas_call(
        functools.partial(direct_kernel, first),
        in_specs=[SMEM] + [VMEM] * (5 if first else 3),
        out_specs=VMEM,
        out_shape=out,
        scratch_shapes=scratch,
        compiler_params=params(20),
    )(live, arrived, occ, virt, *local)


def body(trial_vectors, energy_val, energy_cond, coef_occ, coef_virt, pair_coef, live_aux):
    pair = pair_coef.reshape(2 * CB, NAUX)
    virt = coef_virt.reshape(SLOTS * CB, C)
    cond = energy_cond.reshape(1, CB)

    def exchange(x, axes):
        return lax.all_to_all(x, axes, split_axis=0, concat_axis=0, tiled=True)

    sent, trial, gap, pair = pl.pallas_call(
        first_kernel,
        in_specs=[SMEM] + [HBM] * 4,
        out_specs=[VMEM] * 4,
        out_shape=[
            jax.ShapeDtypeStruct((PAIRS, HALF, 4 * CB + 128), BF16),
            jax.ShapeDtypeStruct((2, K, CB), F32),
            jax.ShapeDtypeStruct((2 * HALF, CB), F32),
            jax.typeof(pair),
        ],
        scratch_shapes=[
            pltpu.VMEM((1, CB), F32),
            pltpu.SMEM((2,), F32),
            pltpu.SemaphoreType.DMA((3 + PARTS,)),
        ],
        cost_estimate=pl.CostEstimate(flops=UNTIL_DIRECT, bytes_accessed=2 * pair.size, transcendentals=0),
        compiler_params=params(8),
    )(live_aux, *(stays(x) for x in (trial_vectors, pair, cond, energy_val)))
    arrived = exchange(sent, ALL)
    sent = direct_call(True, live_aux, arrived, coef_occ, virt, trial, gap)
    arrived = exchange(sent, ALL)
    sent, correction, meet = pl.pallas_call(
        middle_kernel,
        in_specs=[VMEM] * 4,
        out_specs=[VMEM] * 3,
        out_shape=[
            jax.ShapeDtypeStruct((AUX, HALF, 2 * CB + 128), BF16),
            jax.ShapeDtypeStruct((2 * HALF, CB), F32),
            jax.ShapeDtypeStruct((K, 128), F32),
        ],
        compiler_params=params(8),
    )(arrived, pair, trial, gap)
    arrived = exchange(sent, SAME_TR)
    sent = direct_call(False, live_aux, arrived, coef_occ, virt)
    arrived = exchange(sent, ALL)
    mine = pl.pallas_call(
        last_kernel,
        in_specs=[VMEM] * 5,
        out_specs=VMEM,
        out_shape=jax.ShapeDtypeStruct((2 * HALF, CB + 128), F32),
        compiler_params=params(8),
    )(arrived, pair, correction, gap, meet)
    both = lax.all_gather(mine, "grp")
    applied, intersection = pl.pallas_call(
        join_kernel,
        in_specs=[VMEM],
        out_specs=[VMEM] * 2,
        out_shape=[jax.ShapeDtypeStruct((2, K, CB), F32), jax.ShapeDtypeStruct((K, K), F32)],
        compiler_params=params(4),
    )(both)
    return (applied, intersection)


def solution(mesh):
    mesh = Mesh(mesh.devices.reshape(2, 4, 2, 4, TR), ("grp", "y", "zh", "x", "tr"))
    aux = ("y", "zh", "x")
    in_specs = (
        P(aux, None, "tr"),
        P(aux),
        P("tr"),
        P(aux, None, None),
        P(aux, "tr", None),
        P(aux, "tr", None),
        P(aux),
    )
    out_specs = (P(aux, None, "tr"), P())
    return jax.shard_map(body, mesh=mesh, in_specs=in_specs, out_specs=out_specs, check_vma=False)
```

```python
import functools

import jax
import jax.numpy as jnp
from jax import lax
from jax.experimental import pallas as pl
from jax.experimental.pallas import tpu as pltpu
from jax.sharding import Mesh
from jax.sharding import PartitionSpec as P

V = 64
C = 512
K = 8
HALF = 4
AUX = 32
TR = 2
CB = C // TR
PAIRS = AUX * TR
ALL = ("zh", "tr", "y", "x")
SAME_TR = ("zh", "y", "x")
SLOTS = 64
NAUX = 2048
BLOCK = 16
STEPS = SLOTS // BLOCK
PARTS = 4
UNTIL_DIRECT = 2 * 10**10
TILES = NAUX // 128
F32 = jnp.float32
BF16 = jnp.bfloat16
VMEM = pl.BlockSpec(memory_space=pltpu.VMEM)
SMEM = pl.BlockSpec(memory_space=pltpu.SMEM)
HBM = pl.BlockSpec(memory_space=pltpu.HBM)
NT = (((1,), (1,)), ((), ()))


def place(a, t):
    y, zh, x = a // 8, a // 4 % 2, a % 4
    return zh * 32 + t * 16 + y * 4 + x


def place_same_tr(a):
    y, zh, x = a // 8, a // 4 % 2, a % 4
    return zh * 16 + y * 4 + x


def stays(x):
    return pltpu.with_memory_space_constraint(x, pltpu.HBM)


def params(mib):
    return pltpu.CompilerParams(vmem_limit_bytes=mib * 2**20)


def dot(a, b):
    return jnp.dot(a, b, preferred_element_type=F32)


def lane_ids(shape):
    return lax.broadcasted_iota(jnp.int32, shape, len(shape) - 1)


def own_rows(core, rows):
    return jnp.where(core == 0, rows[:HALF], rows[HALF:])


def both_halves(slab):
    parts = [slab[:, CB * i : CB * i + CB] for i in (0, 2, 1, 3)]
    return jnp.concatenate(parts, axis=0)


def first_kernel(
    live_ref, trial_hbm, pair_hbm, cond_hbm, val_hbm, out_ref, trial_ref, gap_ref, pair_ref, cond_ref, val_ref, sems
):
    parts = [pl.ds(2 * CB // PARTS * i, 2 * CB // PARTS) for i in range(PARTS)]
    copies = [
        pltpu.make_async_copy(trial_hbm, trial_ref, sems.at[0]),
        pltpu.make_async_copy(cond_hbm, cond_ref, sems.at[1]),
        pltpu.make_async_copy(val_hbm, val_ref, sems.at[2]),
    ]
    for i in range(PARTS):
        copies.append(pltpu.make_async_copy(pair_hbm.at[parts[i]], pair_ref.at[parts[i]], sems.at[3 + i]))
    for copy in copies:
        copy.start()
    copies[0].wait()
    wide = jnp.concatenate([trial_ref[v].astype(BF16) for v in range(2)], axis=1)
    few = wide.astype(F32)
    few = jnp.concatenate([few[:HALF], few[HALF:]], axis=1).astype(BF16)
    for device in range(PAIRS):
        out_ref[device, :, : 4 * CB] = few
    copies[1].wait()
    copies[2].wait()
    for v in range(2):
        gap_ref[HALF * v : HALF * v + HALF] = jnp.broadcast_to(cond_ref[...] - val_ref[v], (HALF, CB))
    projection = jnp.zeros((K, NAUX), F32)
    for i in range(PARTS):
        copies[3 + i].wait()
        rows = slice(2 * CB // PARTS * i, 2 * CB // PARTS * (i + 1))
        projection += dot(wide[:, rows], pair_ref[rows])
    lanes = lane_ids((HALF, 128))
    for tile in range(TILES):
        part = projection[:, 128 * tile : 128 * tile + 128]
        low, high = part[:HALF], pltpu.roll(part, 64, 1)[HALF:]
        for quarter in range(4):
            both = jnp.where(lanes // 32 == quarter, low, high)
            out_ref[4 * tile + quarter, :, 4 * CB :] = both.astype(BF16)


def direct_kernel(first, *refs):
    if first:
        live_ref, arrived_ref, occ_ref, virt_ref, trial_ref, gap_ref = refs[:6]
        out_ref, rows_ref, vectors_ref, blended_ref, total_ref = refs[6:]
    else:
        live_ref, arrived_ref, occ_ref, virt_ref = refs[:4]
        out_ref, vectors_ref, blended_ref, total_ref = refs[4:]
    core, tr, quarter = lax.axis_index("grp"), lax.axis_index("tr"), lax.axis_index("x")

    row = lax.broadcasted_iota(jnp.int32, (HALF * V, 1), 0)
    if first:
        chosen = lax.broadcasted_iota(jnp.int32, (HALF * V, K * V), 1)
        wanted = K * (row % V) + HALF * core + row // V
        stride = place(0, 1) - place(0, 0)
        wide = [arrived_ref[place(a, 0) + stride * tr].astype(F32) for a in range(AUX)]
        wide = jnp.concatenate([both_halves(slab) for slab in wide], axis=0).astype(BF16)
        projection = jnp.zeros((HALF, 128), F32)
    else:
        chosen = lax.broadcasted_iota(jnp.int32, (HALF * V, HALF * V), 1)
        wanted = HALF * AUX * (row % 2) + HALF * (row % V // 2) + row // V
        slabs = [arrived_ref[place_same_tr(a)].astype(F32) for a in range(AUX)]
        wide = [slabs[a][:, CB * u : CB * u + CB] for u in range(2) for a in range(AUX)]
        wide = jnp.concatenate(wide, axis=0).astype(BF16)
    vectors_ref[...] = dot((chosen == wanted).astype(BF16), wide).astype(BF16)

    live = live_ref[0]
    slot = lax.broadcasted_iota(jnp.int32, (BLOCK * V, V), 0) // V

    def blend(step):
        occ = occ_ref[BLOCK * step : BLOCK * step + BLOCK].reshape(BLOCK * V, V)
        if step > 0:
            occ = jnp.where(slot < live - step * BLOCK, occ, jnp.zeros_like(occ))
        for k in range(HALF):
            piece = dot(occ, vectors_ref[V * k : V * k + V]).astype(BF16)
            for p in range(BLOCK):
                blended_ref[step % 2, V * k : V * k + V, CB * p : CB * p + CB] = piece[V * p : V * p + V]

    blend(0)
    devices = [(a, t) for a in range(AUX) for t in range(TR)]
    for step in range(STEPS):
        rows = slice(step * BLOCK * CB, (step + 1) * BLOCK * CB)
        product = dot(blended_ref[step % 2], virt_ref[rows])
        if step + 1 < STEPS:
            blend(step + 1)
        if first:
            for a, t in devices[step::STEPS]:
                slab = arrived_ref[place(a, t)].astype(F32)
                rows_ref[t, 16 * a : 16 * a + 16] = both_halves(slab).astype(BF16)
                projection += slab[:, 4 * CB :]
        if step == 0:
            total_ref[...] = product
        else:
            total_ref[...] += product

    lanes = lane_ids((K, 128))
    total = total_ref[...].astype(BF16)
    row = lax.broadcasted_iota(jnp.int32, (HALF * AUX, 1), 0)
    chosen = lax.broadcasted_iota(jnp.int32, (HALF * AUX, HALF * V), 1)
    owned = []
    for u in range(2):
        taken = chosen == V * (row % HALF) + 2 * (row // HALF) + u
        owned.append(dot(taken.astype(BF16), total).astype(BF16).astype(F32))
    if first:
        shares = jnp.zeros((K, HALF * V), F32)
        for t in range(TR):
            product = lax.dot_general(
                rows_ref[t], total[:, CB * t : CB * t + CB], NT, preferred_element_type=F32
            ).reshape(V, K, HALF * V)
            mine = lax.broadcasted_iota(jnp.int32, product.shape, 0)
            theirs = lane_ids(product.shape) % V
            shares += jnp.where(mine == theirs, product, 0.0).sum(axis=0)
        group = lane_ids(shares.shape) // V
        kept = jnp.zeros((K, 128), F32)
        for j in range(HALF):
            column = jnp.where(group == j, shares, 0.0).sum(axis=1, keepdims=True)
            for v in range(2):
                vectors = trial_ref[v]
                other = own_rows(core, vectors)[j : j + 1] * gap_ref[HALF * v : HALF * v + 1]
                column += (vectors * other).sum(axis=1, keepdims=True)
            high = column.astype(BF16).astype(F32)
            kept = jnp.where(lanes % 32 == j, high, kept)
            kept = jnp.where(lanes % 32 == HALF + j, column - high, kept)
        ahead = lax.rem(lanes // 32 - quarter + 4, 4)
        kept = jnp.where(ahead < 2, kept, pltpu.roll(kept, 4, 0))[:HALF]
        extra = jnp.where(ahead[:HALF] % 2 == 0, projection, kept)
    else:
        extra = jnp.zeros((HALF, 128), F32)
        for slab in slabs:
            extra += slab[:, 2 * CB :]
    extra = extra.astype(BF16)
    for a in range(AUX):
        for t in range(TR):
            for u in range(2):
                part = owned[u][HALF * a : HALF * a + HALF, CB * t : CB * t + CB]
                out_ref[place(a, t), :, CB * u : CB * u + CB] = part.astype(BF16)
            out_ref[place(a, t), :, 2 * CB :] = extra


def direct_sum(arrived_ref):
    total = jnp.zeros((HALF, 2 * CB), F32)
    for device in range(PAIRS):
        total += arrived_ref[device, :, : 2 * CB].astype(F32)
    return jnp.concatenate([total[:, :CB], total[:, CB:]], axis=0)


def middle_kernel(
    arrived_ref, pair_ref, trial_ref, gap_ref, out_ref, correction_ref, meet_ref
):
    core = lax.axis_index("grp")
    direct = direct_sum(arrived_ref)
    few, lanes = lane_ids((HALF, 128)), lane_ids((K, 128))
    upper = lax.broadcasted_iota(jnp.int32, (K, 128), 0) < HALF
    tiles = []
    sums = [jnp.zeros((HALF, 128), F32) for _ in range(4)]
    for tile in range(TILES):
        low = high = jnp.zeros((HALF, 128), F32)
        for quarter in range(4):
            extra = arrived_ref[4 * tile + quarter, :, 2 * CB :].astype(F32)
            low = jnp.where(few // 32 == quarter, extra, low)
            high = jnp.where(few // 32 == (quarter + 2) % 4, extra, high)
            sums[quarter] += extra
        whole = jnp.concatenate([low, high], axis=0)
        whole = jnp.where(upper, whole, pltpu.roll(whole, 64, 1))
        tiles.append(whole.astype(BF16))
    projection = jnp.concatenate(tiles, axis=1)
    exchange_full = lax.dot_general(projection, pair_ref[...], NT, preferred_element_type=F32)
    mine = own_rows(core, exchange_full)
    exchange = jnp.concatenate([mine[:, :CB], mine[:, CB:]], axis=0)
    low = high = jnp.zeros((HALF, 128), F32)
    for quarter in range(4):
        low = jnp.where(few // 32 == (quarter + 1) % 4, sums[quarter], low)
        high = jnp.where(few // 32 == (quarter + 3) % 4, sums[quarter], high)
    shares = jnp.concatenate([low, high], axis=0)
    meet_exchange = lax.dot_general(projection, projection, NT, preferred_element_type=F32)
    meet = []
    for j in range(HALF):
        column = jnp.where(lanes % 32 % HALF == j, jnp.where(lanes % 32 < K, shares, 0.0), 0.0)
        column = column.sum(axis=1, keepdims=True)
        own = jnp.where(core == 0, meet_exchange[:, j : j + 1], meet_exchange[:, HALF + j : HALF + j + 1])
        meet.append((column + own) / (V * C))
    kept = jnp.zeros((K, 128), F32)
    for j in range(HALF):
        kept = jnp.where(lanes == j, meet[j], kept)
    meet_ref[...] = kept
    gap = gap_ref[...]
    vectors = [trial_ref[v] for v in range(2)]
    trial = jnp.concatenate([own_rows(core, vectors[v]) for v in range(2)], axis=0)
    applied = gap * trial + direct + exchange
    overlap = jnp.concatenate(
        [(vectors[v] * meet[j]).sum(axis=0, keepdims=True) for v in range(2) for j in range(HALF)],
        axis=0,
    )
    correction = (applied - overlap) / gap
    correction_ref[...] = correction
    few = jnp.concatenate([correction[:HALF], correction[HALF:]], axis=1)
    wide = jnp.concatenate([few, jnp.zeros_like(few)], axis=0).astype(BF16)
    projection = dot(wide, pair_ref[...])[:HALF].astype(BF16)
    rounded = few.astype(BF16)
    for a in range(AUX):
        tile = a // 2
        out_ref[a, :, : 2 * CB] = rounded
        out_ref[a, :, 2 * CB :] = projection[:, 128 * tile : 128 * tile + 128]


def last_kernel(arrived_ref, pair_ref, correction_ref, gap_ref, meet_ref, out_ref):
    direct = direct_sum(arrived_ref)
    tiles = []
    for tile in range(TILES):
        at = tile // 8 * 32 + 2 * tile % 16
        tiles.append(arrived_ref[at, :, 2 * CB :].astype(F32) + arrived_ref[at + 16, :, 2 * CB :].astype(F32))
    few = jnp.concatenate(tiles, axis=1)
    projection = jnp.concatenate([few, jnp.zeros_like(few)], axis=0).astype(BF16)
    exchange = lax.dot_general(projection, pair_ref[...], NT, preferred_element_type=F32)
    exchange = jnp.concatenate([exchange[:HALF, :CB], exchange[:HALF, CB:]], axis=0)
    out_ref[:, :CB] = gap_ref[...] * correction_ref[...] + direct + exchange
    out_ref[:, CB:] = meet_ref[...]


def join_kernel(both_ref, applied_ref, meet_ref):
    for v in range(2):
        rows = [both_ref[core, HALF * v : HALF * v + HALF, :CB] for core in range(2)]
        applied_ref[v] = jnp.concatenate(rows, axis=0)
    columns = [both_ref[core, :, CB : CB + HALF] for core in range(2)]
    meet_ref[...] = jnp.concatenate(columns, axis=1)


def direct_call(first, live, arrived, occ, virt, *local):
    out = jax.ShapeDtypeStruct((PAIRS, HALF, 2 * CB + 128), BF16)
    scratch = [
        pltpu.VMEM((HALF * V, CB), BF16),
        pltpu.VMEM((2, HALF * V, BLOCK * CB), BF16),
        pltpu.VMEM((HALF * V, C), F32),
    ]
    if first:
        scratch = [pltpu.VMEM((TR, K * V, CB), BF16), *scratch]
    return pl.pallas_call(
        functools.partial(direct_kernel, first),
        in_specs=[SMEM] + [VMEM] * (5 if first else 3),
        out_specs=VMEM,
        out_shape=out,
        scratch_shapes=scratch,
        compiler_params=params(20),
    )(live, arrived, occ, virt, *local)


def body(trial_vectors, energy_val, energy_cond, coef_occ, coef_virt, pair_coef, live_aux):
    pair = pair_coef.reshape(2 * CB, NAUX)
    virt = coef_virt.reshape(SLOTS * CB, C)
    cond = energy_cond.reshape(1, CB)

    def exchange(x, axes):
        return lax.all_to_all(x, axes, split_axis=0, concat_axis=0, tiled=True)

    sent, trial, gap, pair = pl.pallas_call(
        first_kernel,
        in_specs=[SMEM] + [HBM] * 4,
        out_specs=[VMEM] * 4,
        out_shape=[
            jax.ShapeDtypeStruct((PAIRS, HALF, 4 * CB + 128), BF16),
            jax.ShapeDtypeStruct((2, K, CB), F32),
            jax.ShapeDtypeStruct((2 * HALF, CB), F32),
            jax.typeof(pair),
        ],
        scratch_shapes=[
            pltpu.VMEM((1, CB), F32),
            pltpu.SMEM((2,), F32),
            pltpu.SemaphoreType.DMA((3 + PARTS,)),
        ],
        cost_estimate=pl.CostEstimate(flops=UNTIL_DIRECT, bytes_accessed=2 * pair.size, transcendentals=0),
        compiler_params=params(8),
    )(live_aux, *(stays(x) for x in (trial_vectors, pair, cond, energy_val)))
    arrived = exchange(sent, ALL)
    sent = direct_call(True, live_aux, arrived, coef_occ, virt, trial, gap)
    arrived = exchange(sent, ALL)
    sent, correction, meet = pl.pallas_call(
        middle_kernel,
        in_specs=[VMEM] * 4,
        out_specs=[VMEM] * 3,
        out_shape=[
            jax.ShapeDtypeStruct((AUX, HALF, 2 * CB + 128), BF16),
            jax.ShapeDtypeStruct((2 * HALF, CB), F32),
            jax.ShapeDtypeStruct((K, 128), F32),
        ],
        compiler_params=params(8),
    )(arrived, pair, trial, gap)
    arrived = exchange(sent, SAME_TR)
    sent = direct_call(False, live_aux, arrived, coef_occ, virt)
    arrived = exchange(sent, ALL)
    mine = pl.pallas_call(
        last_kernel,
        in_specs=[VMEM] * 5,
        out_specs=VMEM,
        out_shape=jax.ShapeDtypeStruct((2 * HALF, CB + 128), F32),
        compiler_params=params(8),
    )(arrived, pair, correction, gap, meet)
    both = lax.all_gather(mine, "grp")
    applied, intersection = pl.pallas_call(
        join_kernel,
        in_specs=[VMEM],
        out_specs=[VMEM] * 2,
        out_shape=[jax.ShapeDtypeStruct((2, K, CB), F32), jax.ShapeDtypeStruct((K, K), F32)],
        compiler_params=params(4),
    )(both)
    return (applied, intersection)


def solution(mesh):
    mesh = Mesh(mesh.devices.reshape(2, 4, 2, 4, TR), ("grp", "y", "zh", "x", "tr"))
    aux = ("y", "zh", "x")
    in_specs = (
        P(aux, None, "tr"),
        P(aux),
        P("tr"),
        P(aux, None, None),
        P(aux, "tr", None),
        P(aux, "tr", None),
        P(aux),
    )
    out_specs = (P(aux, None, "tr"), P())
    return jax.shard_map(body, mesh=mesh, in_specs=in_specs, out_specs=out_specs, check_vma=False)
```
